32 devices in a mesh: chan: 8 (over z, y), blk: 4 (over x, core).
Axes of the slice: x: 2, y: 2, z: 4, core: 2. Of those that a mesh axis runs over, the one named last changes fastest.
Arguments:
- voltages: int32 [1024, 262144], P('chan', 'blk'), may hold values from -127 to 127, as said below
Outputs:
- vis_real: float32 [256, 1024, 1024], P(('chan', 'blk'))
- vis_imag: float32 [256, 1024, 1024], P(('chan', 'blk'))
The draws below stay inside these ranges and needn't reach their ends.
Inputs may be any that keep to these rules, and one draw needn't show every extreme that they name: `voltages`: integer voltage samples.
All inputs are finite; a program needn't handle non-finite values.
Results may differ from the reference program's by a relative error of at most 0.004.
Values may be sent and summed in bfloat16 or wider, within the bound.
No kernel may reach another device: no remote copies, remote signals or barrier semaphores. Data moves between devices by JAX's collectives and lax.ppermute only.
A program may use at most 256 MiB of HBM per device.

```python
import math
import jax
import jax.numpy as jnp
from jax import lax

NI = 1024
NC = 256
TAPS = 4
FFT = 512
FRAMES = 512
SAMPLES = 262144


def draw_voltages(key, part):
    key_signal = jax.random.fold_in(key, 101)
    key_sign = jax.random.fold_in(key, 202)
    key_noise = jax.random.fold_in(key, 303)
    signal = jax.random.randint(key_signal, (1, SAMPLES), -40, 41, dtype=jnp.int32)
    polarity = 2 * jax.random.randint(key_sign, (NI, 1), 0, 2, dtype=jnp.int32) - 1
    noise = jax.random.randint(key_noise, (NI, SAMPLES), -87, 88, dtype=jnp.int32)
    return polarity * signal + noise


def setup_inputs(seed: int = 0) -> dict:
    key_list = jax.random.split(jax.random.key(seed), 2)
    voltages = draw_voltages(jax.random.fold_in(key_list[1], 71), 0)
    return dict(voltages=voltages)


def build_taps():
    length = TAPS * FFT
    points = jnp.arange(length, dtype=jnp.float32)
    centre = (length - 1) / 2.0
    window = 0.54 - 0.46 * jnp.cos(2.0 * jnp.pi * points / (length - 1))
    return (jnp.sinc((points - centre) / FFT) * window).reshape(TAPS, FFT)

def spectrum_scale(filter_taps):
    energy = jnp.mean(lax.optimization_barrier(jnp.sum(filter_taps * filter_taps, axis=0)))
    return 1.0 / (56.0 * jnp.sqrt(FFT * energy))

def reference(voltages):
    filter_taps = build_taps()
    scale_factor = spectrum_scale(filter_taps)
    group_size = math.gcd(NI, 16)

    def one_group(group):
        samples = group.astype(jnp.float32).reshape(group_size, FRAMES, FFT)
        padded = jnp.concatenate([jnp.zeros((group_size, TAPS - 1, FFT), jnp.float32), samples], axis=1)
        filtered = jnp.zeros((group_size, FRAMES, FFT), jnp.float32)
        for offset in range(TAPS):
            filtered = filtered + filter_taps[offset] * padded[:, offset:offset + FRAMES, :]
        spectrum = jnp.fft.rfft(filtered, axis=-1)[:, :, :NC]
        real_part = (jnp.real(spectrum) * scale_factor).astype(jnp.bfloat16)
        imag_part = (jnp.imag(spectrum) * scale_factor).astype(jnp.bfloat16)
        return (real_part, imag_part)
    real_all, imag_all = lax.map(one_group, voltages.reshape(NI // group_size, group_size, SAMPLES))
    real_all = jnp.transpose(real_all.reshape(NI, FRAMES, NC), (2, 0, 1))
    imag_all = jnp.transpose(imag_all.reshape(NI, FRAMES, NC), (2, 0, 1))

    def one_channel(planes):
        real_rows = planes[0].astype(jnp.float32)
        imag_rows = planes[1].astype(jnp.float32)
        highest = lax.Precision.HIGHEST
        out_real = jnp.dot(real_rows, real_rows.T, precision=highest) + jnp.dot(imag_rows, imag_rows.T, precision=highest)
        out_imag = jnp.dot(imag_rows, real_rows.T, precision=highest) - jnp.dot(real_rows, imag_rows.T, precision=highest)
        return (out_real / FRAMES, out_imag / FRAMES)
    vis_real, vis_imag = lax.map(one_channel, (real_all, imag_all))
    return (vis_real, vis_imag)
```

```python
import functools

import jax
import jax.numpy as jnp
import numpy as np
from jax import lax
from jax.experimental import pallas as pl
from jax.experimental.pallas import tpu as pltpu
from jax.sharding import PartitionSpec as P

NC = 256
TAPS = 4
FFT = 512
HISTORY = TAPS - 1
FRAME_BLOCK = 16
ROWS = 16
VMEM_LIMIT = 56 * 1024 * 1024


def shifted(value, axis, steps):
    count = lax.axis_size(axis)
    leading, last = (max(0, -steps), min(count, count - steps))
    return lax.ppermute(value, axis, [(source, source + steps) for source in range(leading, last)])


def build_taps():
    length = TAPS * FFT
    points = np.arange(length, dtype=np.float64)
    window = 0.54 - 0.46 * np.cos(2.0 * np.pi * points / (length - 1))
    return (np.sinc((points - (length - 1) / 2.0) / FFT) * window).reshape(TAPS, FFT)


def spectrum_scale(filter_taps):
    energy = np.mean(np.sum(filter_taps * filter_taps, axis=0))
    return 1.0 / (56.0 * np.sqrt(FFT * energy))


def build_transform(chunks, devices, chan_local, folds):
    scale = spectrum_scale(build_taps())
    points = np.arange(FFT // folds)
    rows = []
    for chunk in chunks:
        channel = np.arange(devices) * chan_local + chunk
        angle = (channel[:, None] * points[None, :] % FFT) * (2.0 * np.pi / FFT)
        rows.append(np.stack([np.cos(angle), -np.sin(angle)], axis=1))
    matrix = (np.concatenate(rows) * scale).reshape(-1, FFT // folds).astype(np.float32)
    high = matrix.astype(jnp.bfloat16)
    low = (matrix - high.astype(np.float32)).astype(jnp.bfloat16)
    return np.concatenate([high, high, low], axis=1)


def spectra_kernel(groups, folds, *refs):
    chunk_count = sum(len(chunks) for _, chunks in groups)
    voltages, halo, taps = refs[:3]
    transforms = refs[3 : 3 + len(groups)]
    outputs = refs[3 + len(groups) : 3 + len(groups) + chunk_count]
    history, turned = refs[3 + len(groups) + chunk_count :][:2]
    folded = refs[3 + len(groups) + chunk_count + 2 :]
    inputs_here = voltages.shape[0]
    part = FFT // folds
    lanes = 128

    @pl.when(pl.program_id(0) == 0)
    def _():
        history[...] = halo[...].astype(jnp.float32)

    def filter_rows(step, carry):
        rows = pl.ds(pl.multiple_of(step * ROWS, ROWS), ROWS)
        for start in range(0, part, lanes):
            pieces = []
            for fold in range(folds):
                column = fold * part + start
                weights = [taps[offset : offset + 1, column : column + lanes] for offset in range(TAPS)]
                past = [history[rows, frame * FFT + column : frame * FFT + column + lanes] for frame in range(HISTORY)]
                filtered = []
                for frame in range(FRAME_BLOCK):
                    at = frame * FFT + column
                    past.append(voltages[rows, at : at + lanes].astype(jnp.float32))
                    value = weights[0] * past[0]
                    for offset in range(1, TAPS):
                        value = value + weights[offset] * past[offset]
                    filtered.append(value)
                    past = past[1:]
                for frame in range(HISTORY):
                    history[rows, frame * FFT + column : frame * FFT + column + lanes] = past[frame]
                pieces.append(filtered)
            for frame in range(FRAME_BLOCK):
                for (residue, _), target in zip(groups, folded):
                    value = pieces[0][frame]
                    if folds == 2:
                        value = value + pieces[1][frame] if residue == 0 else value - pieces[1][frame]
                    high = value.astype(jnp.bfloat16)
                    low = (value - high.astype(jnp.float32)).astype(jnp.bfloat16)
                    at = pl.ds(pl.multiple_of(frame * inputs_here + step * ROWS, ROWS), ROWS)
                    target[at, start : start + lanes] = high
                    target[at, part + start : part + start + lanes] = low
                    target[at, 2 * part + start : 2 * part + start + lanes] = high
        return carry

    lax.fori_loop(0, inputs_here // ROWS, filter_rows, 0)

    position = 0
    for (_, chunks), transform, source in zip(groups, transforms, folded):
        per_chunk = transform.shape[0] // len(chunks)
        batch = max(1, min(FRAME_BLOCK, 256 // inputs_here)) if inputs_here >= lanes else 1
        for first in range(0, FRAME_BLOCK, batch):
            result = lax.dot_general(
                transform[...],
                source[first * inputs_here : (first + batch) * inputs_here, :],
                (((1,), (1,)), ((), ())),
                preferred_element_type=jnp.float32,
            )
            for frame in range(batch):
                turned[pl.ds(first + frame, transform.shape[0], stride=FRAME_BLOCK), :] = result[
                    :, frame * inputs_here : (frame + 1) * inputs_here
                ]
        for index in range(len(chunks)):
            start = index * per_chunk * FRAME_BLOCK
            block = turned[start : start + per_chunk * FRAME_BLOCK, :]
            outputs[position][...] = block.reshape(outputs[position].shape).astype(jnp.bfloat16)
            position += 1


def spectra(voltages, halo, chunks, devices, chan_local):
    folds = 2 if chan_local % 2 == 0 else 1
    inputs_here = voltages.shape[0]
    frames_dev = voltages.shape[1] // FFT
    groups = []
    for residue in range(folds):
        members = [chunk for chunk in chunks if chunk % folds == residue]
        if members:
            groups.append((residue, members))
    transforms = [jnp.asarray(build_transform(members, devices, chan_local, folds)) for _, members in groups]
    order = [chunk for _, members in groups for chunk in members]
    shape = (devices, 2, frames_dev, inputs_here)
    block = (devices, 2, FRAME_BLOCK, inputs_here)
    depth = 3 * (FFT // folds)
    most = max(transform.shape[0] for transform in transforms)
    results = pl.pallas_call(
        functools.partial(spectra_kernel, groups, folds),
        grid=(frames_dev // FRAME_BLOCK,),
        in_specs=[
            pl.BlockSpec((inputs_here, FRAME_BLOCK * FFT), lambda step: (0, step)),
            pl.BlockSpec((inputs_here, HISTORY * FFT), lambda step: (0, 0)),
            pl.BlockSpec((TAPS, FFT), lambda step: (0, 0)),
        ]
        + [pl.BlockSpec(transform.shape, lambda step: (0, 0)) for transform in transforms],
        out_specs=[pl.BlockSpec(block, lambda step: (0, 0, step, 0)) for _ in order],
        out_shape=[jax.ShapeDtypeStruct(shape, jnp.bfloat16) for _ in order],
        scratch_shapes=[
            pltpu.VMEM((inputs_here, HISTORY * FFT), jnp.float32),
            pltpu.VMEM((most * FRAME_BLOCK, inputs_here), jnp.float32),
        ]
        + [pltpu.VMEM((FRAME_BLOCK * inputs_here, depth), jnp.bfloat16) for _ in groups],
        compiler_params=pltpu.CompilerParams(vmem_limit_bytes=VMEM_LIMIT),
        cost_estimate=pl.CostEstimate(
            flops=2 * frames_dev * inputs_here * depth * sum(transform.shape[0] for transform in transforms),
            bytes_accessed=voltages.size * 4 + 2 * len(order) * int(np.prod(shape)),
            transcendentals=0,
        ),
        name="spectra",
    )(voltages, halo, jnp.asarray(build_taps().astype(np.float32)), *transforms)
    return dict(zip(order, results))


def visibility_kernel(received, *refs):
    real_out, imag_out, across, turned, swapped = refs[-5:]
    chan_count, blk_count, _, frames_dev, inputs_here = received.shape
    depth = blk_count * 2 * frames_dev
    total_frames = blk_count * frames_dev
    row_block = real_out.shape[1]

    @pl.when(pl.program_id(0) == 0)
    def _():
        for chan in range(chan_count):
            across[:, chan * inputs_here : (chan + 1) * inputs_here] = received[chan].reshape(depth, inputs_here)

    start = pl.multiple_of(pl.program_id(0) * row_block, row_block)
    turned[...] = across[:, pl.ds(start, row_block)].T
    for blk in range(blk_count):
        at = blk * 2 * frames_dev
        swapped[:, at : at + frames_dev] = turned[:, at + frames_dev : at + 2 * frames_dev]
        swapped[:, at + frames_dev : at + 2 * frames_dev] = -turned[:, at : at + frames_dev]
    everything = across[...]
    real_out[0] = jnp.dot(turned[...], everything, preferred_element_type=jnp.float32) / total_frames
    imag_out[0] = jnp.dot(swapped[...], everything, preferred_element_type=jnp.float32) / total_frames


def visibilities(received, before, chunk, chan_local):
    chan_count, blk_count, _, frames_dev, inputs_here = received.shape
    inputs = chan_count * inputs_here
    depth = blk_count * 2 * frames_dev
    row_block = 256
    shape = jax.ShapeDtypeStruct((chan_local, inputs, inputs), jnp.float32)
    out_spec = pl.BlockSpec((1, row_block, inputs), lambda step: (chunk, step, 0))
    return pl.pallas_call(
        visibility_kernel,
        grid=(inputs // row_block,),
        in_specs=[pl.BlockSpec(received.shape, lambda step: (0, 0, 0, 0, 0))]
        + [pl.BlockSpec(memory_space=pl.ANY) for _ in before],
        out_specs=[out_spec, out_spec],
        out_shape=[shape, shape],
        input_output_aliases={1 + index: index for index in range(len(before))},
        scratch_shapes=[
            pltpu.VMEM((depth, inputs), jnp.bfloat16),
            pltpu.VMEM((row_block, depth), jnp.bfloat16),
            pltpu.VMEM((row_block, depth), jnp.bfloat16),
        ],
        compiler_params=pltpu.CompilerParams(vmem_limit_bytes=VMEM_LIMIT),
        cost_estimate=pl.CostEstimate(
            flops=4 * inputs * inputs * depth,
            bytes_accessed=2 * received.size + 8 * inputs * inputs,
            transcendentals=0,
        ),
        name="visibilities",
    )(received, *before)


def local(voltages):
    inputs_here = voltages.shape[0]
    frames_dev = voltages.shape[1] // FFT
    chan_count = lax.axis_size("chan")
    blk_count = lax.axis_size("blk")
    devices = chan_count * blk_count
    chan_local = NC // devices
    tail = voltages[:, (frames_dev - HISTORY) * FFT :].astype(jnp.bfloat16)
    halo = shifted(tail, "blk", 1)
    first = [0]
    rest = list(range(1, chan_local))
    sent = spectra(voltages, halo, first, devices, chan_local)
    if rest:
        sent.update(spectra(voltages, halo, rest, devices, chan_local))
    outputs = ()
    for chunk in range(chan_local):
        received = lax.all_to_all(sent[chunk], ("chan", "blk"), split_axis=0, concat_axis=0, tiled=True)
        received = received.reshape(chan_count, blk_count, 2, frames_dev, inputs_here)
        outputs = visibilities(received, outputs, chunk, chan_local)
    return tuple(outputs)


def solution(mesh):
    return jax.shard_map(
        local,
        mesh=mesh,
        in_specs=(P("chan", "blk"),),
        out_specs=(P(("chan", "blk"), None, None), P(("chan", "blk"), None, None)),
        check_vma=False,
    )
```

```python
import functools

import jax
import jax.numpy as jnp
import numpy as np
from jax import lax
from jax.experimental import pallas as pl
from jax.experimental.pallas import tpu as pltpu
from jax.sharding import PartitionSpec as P

NC = 256
TAPS = 4
FFT = 512
HISTORY = TAPS - 1
FRAME_BLOCK = 16
ROWS = 16
VMEM_LIMIT = 56 * 1024 * 1024


def shifted(value, axis, steps):
    count = lax.axis_size(axis)
    leading, last = (max(0, -steps), min(count, count - steps))
    return lax.ppermute(value, axis, [(source, source + steps) for source in range(leading, last)])


def build_taps():
    length = TAPS * FFT
    points = np.arange(length, dtype=np.float64)
    window = 0.54 - 0.46 * np.cos(2.0 * np.pi * points / (length - 1))
    return (np.sinc((points - (length - 1) / 2.0) / FFT) * window).reshape(TAPS, FFT)


def spectrum_scale(filter_taps):
    energy = np.mean(np.sum(filter_taps * filter_taps, axis=0))
    return 1.0 / (56.0 * np.sqrt(FFT * energy))


def build_dft(channels, devices, chan_local, points):
    rows = []
    for channel in channels:
        whole = np.arange(devices) * chan_local + channel
        angle = (whole[:, None] * np.arange(points)[None, :] % FFT) * (2.0 * np.pi / FFT)
        rows.append(np.stack([np.cos(angle), -np.sin(angle)], axis=1))
    return (np.concatenate(rows) * spectrum_scale(build_taps())).reshape(-1, points)


def split_high_low(matrix):
    matrix = matrix.astype(np.float32)
    high = matrix.astype(jnp.bfloat16)
    return high, (matrix - high.astype(np.float32)).astype(jnp.bfloat16)


def build_transform(channels, devices, chan_local, folds):
    high, low = split_high_low(build_dft(channels, devices, chan_local, FFT // folds))
    return np.concatenate([high, high, low], axis=1)


def build_direct(channel, devices, chan_local):
    matrix = build_dft([channel], devices, chan_local, FFT)
    high, low = split_high_low(np.concatenate([matrix * taps[None, :] for taps in build_taps()]))
    return np.concatenate([high, low], axis=0)


def direct_kernel(voltages, halo, transform, *refs):
    output, products, turned = refs[-3:]
    inputs_here = voltages.shape[0]
    rows = turned.shape[0] // FRAME_BLOCK
    batch = 2 if inputs_here == 128 else 1

    def multiply(target, source, frames):
        for first in range(0, frames, batch):
            count = min(batch, frames - first)
            frame_list = [source[:, frame * FFT : (frame + 1) * FFT] for frame in range(first, first + count)]
            samples = jnp.concatenate(frame_list, axis=0).astype(jnp.float32).astype(jnp.bfloat16)
            result = lax.dot_general(
                transform[...], samples, (((1,), (1,)), ((), ())), preferred_element_type=jnp.float32
            )
            for frame in range(count):
                products[target + first + frame] = result[:, frame * inputs_here : (frame + 1) * inputs_here]

    @pl.when(pl.program_id(0) == 0)
    def _():
        multiply(0, halo, HISTORY)

    multiply(HISTORY, voltages, FRAME_BLOCK)
    for frame in range(FRAME_BLOCK):
        total = None
        for part in (1, 0):
            for offset in range(TAPS):
                start = (part * TAPS + offset) * rows
                term = products[frame + offset, start : start + rows, :]
                total = term if total is None else total + term
        turned[pl.ds(frame, rows, stride=FRAME_BLOCK), :] = total
    for frame in range(HISTORY):
        products[frame] = products[FRAME_BLOCK + frame]
    output[...] = turned[...].reshape(output.shape).astype(jnp.bfloat16)


def direct_spectra(voltages, halo, before, channel, blocks, devices, chan_local):
    inputs_here = voltages.shape[0]
    frames_dev = voltages.shape[1] // FFT
    transform = jnp.asarray(build_direct(channel, devices, chan_local))
    shape = (devices, 1, 2, frames_dev, inputs_here)
    return pl.pallas_call(
        direct_kernel,
        grid=(blocks,),
        in_specs=[
            pl.BlockSpec((inputs_here, FRAME_BLOCK * FFT), lambda step: (0, step)),
            pl.BlockSpec((inputs_here, HISTORY * FFT), lambda step: (0, 0)),
            pl.BlockSpec(transform.shape, lambda step: (0, 0)),
        ]
        + [pl.BlockSpec(memory_space=pl.ANY) for _ in before],
        out_specs=pl.BlockSpec((devices, 1, 2, FRAME_BLOCK, inputs_here), lambda step: (0, 0, 0, step, 0)),
        out_shape=jax.ShapeDtypeStruct(shape, jnp.bfloat16),
        input_output_aliases={3: 0} if before else {},
        scratch_shapes=[
            pltpu.VMEM((HISTORY + FRAME_BLOCK, transform.shape[0], inputs_here), jnp.float32),
            pltpu.VMEM((devices * 2 * FRAME_BLOCK, inputs_here), jnp.float32),
        ],
        compiler_params=pltpu.CompilerParams(vmem_limit_bytes=VMEM_LIMIT),
        cost_estimate=pl.CostEstimate(
            flops=2 * blocks * FRAME_BLOCK * inputs_here * FFT * transform.shape[0],
            bytes_accessed=blocks * FRAME_BLOCK * inputs_here * (4 * FFT + 4 * devices),
            transcendentals=0,
        ),
        name="direct_spectra",
    )(voltages, halo, transform, *before)


def spectra_kernel(groups, folds, places, chunk_count, *refs):
    voltages, halo, taps = refs[:3]
    transforms = refs[3 : 3 + len(groups)]
    outputs = refs[3 + len(groups) : 3 + len(groups) + chunk_count]
    history, turned = refs[3 + len(groups) + chunk_count :][:2]
    folded = refs[3 + len(groups) + chunk_count + 2 :]
    inputs_here = voltages.shape[0]
    part = FFT // folds
    lanes = 128

    @pl.when(pl.program_id(0) == 0)
    def _():
        history[...] = halo[...].astype(jnp.float32)

    def filter_rows(step, carry):
        rows = pl.ds(pl.multiple_of(step * ROWS, ROWS), ROWS)
        for start in range(0, part, lanes):
            pieces = []
            for fold in range(folds):
                column = fold * part + start
                weights = [taps[offset : offset + 1, column : column + lanes] for offset in range(TAPS)]
                past = [history[rows, frame * FFT + column : frame * FFT + column + lanes] for frame in range(HISTORY)]
                filtered = []
                for frame in range(FRAME_BLOCK):
                    at = frame * FFT + column
                    past.append(voltages[rows, at : at + lanes].astype(jnp.float32))
                    value = weights[0] * past[0]
                    for offset in range(1, TAPS):
                        value = value + weights[offset] * past[offset]
                    filtered.append(value)
                    past = past[1:]
                for frame in range(HISTORY):
                    history[rows, frame * FFT + column : frame * FFT + column + lanes] = past[frame]
                pieces.append(filtered)
            for frame in range(FRAME_BLOCK):
                for (residue, _), target in zip(groups, folded):
                    value = pieces[0][frame]
                    if folds == 2:
                        value = value + pieces[1][frame] if residue == 0 else value - pieces[1][frame]
                    high = value.astype(jnp.bfloat16)
                    low = (value - high.astype(jnp.float32)).astype(jnp.bfloat16)
                    at = pl.ds(pl.multiple_of(frame * inputs_here + step * ROWS, ROWS), ROWS)
                    target[at, start : start + lanes] = high
                    target[at, part + start : part + start + lanes] = low
                    target[at, 2 * part + start : 2 * part + start + lanes] = high
        return carry

    lax.fori_loop(0, inputs_here // ROWS, filter_rows, 0)

    for (_, channels), transform, source in zip(groups, transforms, folded):
        per_channel = transform.shape[0] // len(channels)
        batch = max(1, min(FRAME_BLOCK, 256 // inputs_here)) if inputs_here >= lanes else 1
        for first in range(0, FRAME_BLOCK, batch):
            result = lax.dot_general(
                transform[...],
                source[first * inputs_here : (first + batch) * inputs_here, :],
                (((1,), (1,)), ((), ())),
                preferred_element_type=jnp.float32,
            )
            for frame in range(batch):
                turned[pl.ds(first + frame, transform.shape[0], stride=FRAME_BLOCK), :] = result[
                    :, frame * inputs_here : (frame + 1) * inputs_here
                ]
        for index, channel in enumerate(channels):
            start = index * per_channel * FRAME_BLOCK
            block = turned[start : start + per_channel * FRAME_BLOCK, :]
            chunk, slot = places[channel]
            block = block.reshape(per_channel // 2, 2, FRAME_BLOCK, inputs_here)
            outputs[chunk][:, slot] = block.astype(jnp.bfloat16)


def spectra(voltages, halo, chunks, devices, chan_local):
    folds = 2 if chan_local % 2 == 0 else 1
    inputs_here = voltages.shape[0]
    frames_dev = voltages.shape[1] // FFT
    places = {channel: (index, slot) for index, chunk in enumerate(chunks) for slot, channel in enumerate(chunk)}
    groups = []
    for residue in range(folds):
        members = [channel for channel in sorted(places) if channel % folds == residue]
        if members:
            groups.append((residue, members))
    transforms = [jnp.asarray(build_transform(members, devices, chan_local, folds)) for _, members in groups]
    depth = 3 * (FFT // folds)
    most = max(transform.shape[0] for transform in transforms)
    return pl.pallas_call(
        functools.partial(spectra_kernel, groups, folds, places, len(chunks)),
        grid=(frames_dev // FRAME_BLOCK,),
        in_specs=[
            pl.BlockSpec((inputs_here, FRAME_BLOCK * FFT), lambda step: (0, step)),
            pl.BlockSpec((inputs_here, HISTORY * FFT), lambda step: (0, 0)),
            pl.BlockSpec((TAPS, FFT), lambda step: (0, 0)),
        ]
        + [pl.BlockSpec(transform.shape, lambda step: (0, 0)) for transform in transforms],
        out_specs=[
            pl.BlockSpec((devices, len(chunk), 2, FRAME_BLOCK, inputs_here), lambda step: (0, 0, 0, step, 0))
            for chunk in chunks
        ],
        out_shape=[
            jax.ShapeDtypeStruct((devices, len(chunk), 2, frames_dev, inputs_here), jnp.bfloat16) for chunk in chunks
        ],
        scratch_shapes=[
            pltpu.VMEM((inputs_here, HISTORY * FFT), jnp.float32),
            pltpu.VMEM((most * FRAME_BLOCK, inputs_here), jnp.float32),
        ]
        + [pltpu.VMEM((FRAME_BLOCK * inputs_here, depth), jnp.bfloat16) for _ in groups],
        compiler_params=pltpu.CompilerParams(vmem_limit_bytes=VMEM_LIMIT),
        cost_estimate=pl.CostEstimate(
            flops=2 * frames_dev * inputs_here * depth * sum(transform.shape[0] for transform in transforms),
            bytes_accessed=frames_dev * inputs_here * (4 * FFT + 4 * devices * len(places)),
            transcendentals=0,
        ),
        name="spectra",
    )(voltages, halo, jnp.asarray(build_taps().astype(np.float32)), *transforms)


def visibility_kernel(carried, received, *refs):
    across, turned, swapped = refs[-3:]
    real_out, imag_out = refs[-5 - carried : -3 - carried]
    chan_count, blk_count, _, _, frames_dev, inputs_here = received.shape
    depth = blk_count * 2 * frames_dev
    total_frames = blk_count * frames_dev
    row_block = real_out.shape[1]

    @pl.when(pl.program_id(1) == 0)
    def _():
        for chan in range(chan_count):
            across[:, chan * inputs_here : (chan + 1) * inputs_here] = received[chan].reshape(depth, inputs_here)

    start = pl.multiple_of(pl.program_id(1) * row_block, row_block)
    turned[...] = across[:, pl.ds(start, row_block)].T
    for blk in range(blk_count):
        at = blk * 2 * frames_dev
        swapped[:, at : at + frames_dev] = turned[:, at + frames_dev : at + 2 * frames_dev]
        swapped[:, at + frames_dev : at + 2 * frames_dev] = -turned[:, at : at + frames_dev]
    everything = across[...]
    real_out[0] = jnp.dot(turned[...], everything, preferred_element_type=jnp.float32) / total_frames
    imag_out[0] = jnp.dot(swapped[...], everything, preferred_element_type=jnp.float32) / total_frames


def visibilities(received, before, carry, chunk, chan_local):
    chan_count, blk_count, channels, _, frames_dev, inputs_here = received.shape
    inputs = chan_count * inputs_here
    depth = blk_count * 2 * frames_dev
    row_block = 256
    shape = jax.ShapeDtypeStruct((chan_local, inputs, inputs), jnp.float32)
    out_spec = pl.BlockSpec((1, row_block, inputs), lambda channel, step: (chunk[0] + channel, step, 0))
    anywhere = pl.BlockSpec(memory_space=pl.ANY)
    aliases = {1 + index: index for index in range(len(before))}
    aliases.update({1 + len(before) + index: 2 + index for index in range(len(carry))})
    results = pl.pallas_call(
        functools.partial(visibility_kernel, len(carry)),
        grid=(channels, inputs // row_block),
        in_specs=[
            pl.BlockSpec(
                (chan_count, blk_count, 1, 2, frames_dev, inputs_here), lambda channel, step: (0, 0, channel, 0, 0, 0)
            )
        ]
        + [anywhere for _ in before]
        + [anywhere for _ in carry],
        out_specs=[out_spec, out_spec] + [anywhere for _ in carry],
        out_shape=[shape, shape] + [jax.ShapeDtypeStruct(array.shape, array.dtype) for array in carry],
        input_output_aliases=aliases,
        scratch_shapes=[
            pltpu.VMEM((depth, inputs), jnp.bfloat16),
            pltpu.VMEM((row_block, depth), jnp.bfloat16),
            pltpu.VMEM((row_block, depth), jnp.bfloat16),
        ],
        compiler_params=pltpu.CompilerParams(vmem_limit_bytes=VMEM_LIMIT),
        cost_estimate=pl.CostEstimate(
            flops=4 * channels * inputs * inputs * depth,
            bytes_accessed=2 * received.size + 8 * channels * inputs * inputs,
            transcendentals=0,
        ),
        name="visibilities",
    )(received, *before, *carry)
    return tuple(results[:2]), list(results[2:])


def split_channels(chan_local):
    if chan_local < 4:
        return [[channel] for channel in range(chan_local)]
    middle = list(range(1, chan_local - 1))
    return [[0]] + [middle[start : start + 2] for start in range(0, len(middle), 2)] + [[chan_local - 1]]


def local(voltages):
    inputs_here = voltages.shape[0]
    frames_dev = voltages.shape[1] // FFT
    chan_count = lax.axis_size("chan")
    blk_count = lax.axis_size("blk")
    devices = chan_count * blk_count
    chan_local = NC // devices
    tail = voltages[:, (frames_dev - HISTORY) * FFT :].astype(jnp.bfloat16)
    halo = shifted(tail, "blk", 1)
    chunks = split_channels(chan_local)
    if len(chunks) > 1:
        nothing = jnp.zeros_like(tail)
        early = direct_spectra(voltages, nothing, [], 0, frames_dev // FRAME_BLOCK, devices, chan_local)
        sent = [direct_spectra(voltages, halo, [early], 0, 1, devices, chan_local)]
        sent += spectra(voltages, halo, chunks[1:], devices, chan_local)
    else:
        sent = spectra(voltages, halo, chunks, devices, chan_local)
    outputs = ()
    received = []
    for index, chunk in enumerate(chunks):
        if index >= 2:
            outputs, carried = visibilities(received[index - 2], outputs, [sent[index]], chunks[index - 2], chan_local)
            sent[index] = carried[0]
        arrived = lax.all_to_all(sent[index], ("chan", "blk"), split_axis=0, concat_axis=0, tiled=True)
        received.append(arrived.reshape(chan_count, blk_count, len(chunk), 2, frames_dev, inputs_here))
    for index in range(max(0, len(chunks) - 2), len(chunks)):
        outputs, _ = visibilities(received[index], outputs, [], chunks[index], chan_local)
    return tuple(outputs)


def solution(mesh):
    return jax.shard_map(
        local,
        mesh=mesh,
        in_specs=(P("chan", "blk"),),
        out_specs=(P(("chan", "blk"), None, None), P(("chan", "blk"), None, None)),
        check_vma=False,
    )
```

```python
import functools

import jax
import jax.numpy as jnp
import numpy as np
from jax import lax
from jax.experimental import pallas as pl
from jax.experimental.pallas import tpu as pltpu
from jax.sharding import PartitionSpec as P

NC = 256
TAPS = 4
FFT = 512
HISTORY = TAPS - 1
FRAME_BLOCK = 16
ROWS = 16
VMEM_LIMIT = 56 * 1024 * 1024
VISIBILITY_LIMIT = 40 * 1024 * 1024


def shifted(value, axis, steps):
    count = lax.axis_size(axis)
    leading, last = (max(0, -steps), min(count, count - steps))
    return lax.ppermute(value, axis, [(source, source + steps) for source in range(leading, last)])


def build_taps():
    length = TAPS * FFT
    points = np.arange(length, dtype=np.float64)
    window = 0.54 - 0.46 * np.cos(2.0 * np.pi * points / (length - 1))
    return (np.sinc((points - (length - 1) / 2.0) / FFT) * window).reshape(TAPS, FFT)


def spectrum_scale(filter_taps):
    energy = np.mean(np.sum(filter_taps * filter_taps, axis=0))
    return 1.0 / (56.0 * np.sqrt(FFT * energy))


def build_dft(channels, devices, chan_local, points):
    rows = []
    for channel in channels:
        whole = np.arange(devices) * chan_local + channel
        angle = (whole[:, None] * np.arange(points)[None, :] % FFT) * (2.0 * np.pi / FFT)
        rows.append(np.stack([np.cos(angle), -np.sin(angle)], axis=1))
    return (np.concatenate(rows) * spectrum_scale(build_taps())).reshape(-1, points)


def split_high_low(matrix):
    matrix = matrix.astype(np.float32)
    high = matrix.astype(jnp.bfloat16)
    return high, (matrix - high.astype(np.float32)).astype(jnp.bfloat16)


def build_transform(channels, devices, chan_local, folds):
    high, low = split_high_low(build_dft(channels, devices, chan_local, FFT // folds))
    return np.concatenate([high, high, low], axis=1)


def build_direct(channel, devices, chan_local):
    matrix = build_dft([channel], devices, chan_local, FFT)
    high, low = split_high_low(np.concatenate([matrix * taps[None, :] for taps in build_taps()]))
    return np.concatenate([high, low], axis=0)


def history_specs(history, inputs_here, first_block):
    if len(history) == 1:
        return [pl.BlockSpec((inputs_here, HISTORY * FFT), lambda step: (0, 0))]
    before = first_block * FRAME_BLOCK - HISTORY
    return [pl.BlockSpec((inputs_here, FFT), functools.partial(lambda at, step: (0, at), before + k)) for k in range(HISTORY)]


def direct_kernel(history_count, voltages, *refs):
    history = refs[:history_count]
    transform, output, tail, products, turned = refs[history_count:]
    inputs_here = voltages.shape[0]
    rows = turned.shape[0] // FRAME_BLOCK
    batch = 2 if inputs_here == 128 else 1

    def multiply(target, frames):
        for first in range(0, len(frames), batch):
            group = [source[:, at : at + FFT] for source, at in frames[first : first + batch]]
            samples = jnp.concatenate(group, axis=0).astype(jnp.float32).astype(jnp.bfloat16)
            result = lax.dot_general(
                transform[...], samples, (((1,), (1,)), ((), ())), preferred_element_type=jnp.float32
            )
            for frame in range(len(group)):
                products[target + first + frame] = result[:, frame * inputs_here : (frame + 1) * inputs_here]

    @pl.when(pl.program_id(0) == 0)
    def _():
        multiply(0, [(source, 0) for source in history])

    multiply(HISTORY, [(voltages, frame * FFT) for frame in range(FRAME_BLOCK)])
    for frame in range(FRAME_BLOCK):
        total = None
        for part in (1, 0):
            for offset in range(TAPS):
                start = (part * TAPS + offset) * rows
                term = products[frame + offset, start : start + rows, :]
                total = term if total is None else total + term
        turned[pl.ds(frame, rows, stride=FRAME_BLOCK), :] = total
    for frame in range(HISTORY):
        products[frame] = products[FRAME_BLOCK + frame]
    output[...] = turned[...].reshape(output.shape).astype(jnp.bfloat16)

    @pl.when(pl.program_id(0) == pl.num_programs(0) - 1)
    def _():
        tail[...] = voltages[:, (FRAME_BLOCK - HISTORY) * FFT :].astype(jnp.float32).astype(jnp.bfloat16)


def direct_spectra(voltages, channel, first_block, devices, chan_local):
    inputs_here = voltages.shape[0]
    frames = voltages.shape[1] // FFT - first_block * FRAME_BLOCK
    transform = jnp.asarray(build_direct(channel, devices, chan_local))
    history = [voltages] * HISTORY
    return pl.pallas_call(
        functools.partial(direct_kernel, len(history)),
        grid=(frames // FRAME_BLOCK,),
        in_specs=[pl.BlockSpec((inputs_here, FRAME_BLOCK * FFT), lambda step: (0, first_block + step))]
        + history_specs(history, inputs_here, first_block)
        + [pl.BlockSpec(transform.shape, lambda step: (0, 0))],
        out_specs=[
            pl.BlockSpec((devices, 1, 2, FRAME_BLOCK, inputs_here), lambda step: (0, 0, 0, step, 0)),
            pl.BlockSpec((inputs_here, HISTORY * FFT), lambda step: (0, 0)),
        ],
        out_shape=[
            jax.ShapeDtypeStruct((devices, 1, 2, frames, inputs_here), jnp.bfloat16),
            jax.ShapeDtypeStruct((inputs_here, HISTORY * FFT), jnp.bfloat16),
        ],
        scratch_shapes=[
            pltpu.VMEM((HISTORY + FRAME_BLOCK, transform.shape[0], inputs_here), jnp.float32),
            pltpu.VMEM((devices * 2 * FRAME_BLOCK, inputs_here), jnp.float32),
        ],
        compiler_params=pltpu.CompilerParams(vmem_limit_bytes=VMEM_LIMIT),
        cost_estimate=pl.CostEstimate(
            flops=2 * frames * inputs_here * FFT * transform.shape[0],
            bytes_accessed=frames * inputs_here * (4 * FFT + 4 * devices),
            transcendentals=0,
        ),
        name="direct_spectra",
    )(voltages, *history, transform)


def spectra_kernel(groups, folds, places, history_count, array_count, voltages, *refs):
    before = refs[:history_count]
    taps = refs[history_count]
    transforms = refs[history_count + 1 : history_count + 1 + len(groups)]
    history, turned = refs[-2 - len(groups) : len(refs) - len(groups)]
    folded = refs[len(refs) - len(groups) :]
    outputs = refs[-2 - len(groups) - array_count : -2 - len(groups)]
    inputs_here = voltages.shape[0]
    part = FFT // folds
    lanes = 128

    @pl.when(pl.program_id(0) == 0)
    def _():
        at = 0
        for source in before:
            history[:, at : at + source.shape[1]] = source[...].astype(jnp.float32)
            at += source.shape[1]

    def filter_rows(step, carry):
        rows = pl.ds(pl.multiple_of(step * ROWS, ROWS), ROWS)
        for start in range(0, part, lanes):
            pieces = []
            for fold in range(folds):
                column = fold * part + start
                weights = [taps[offset : offset + 1, column : column + lanes] for offset in range(TAPS)]
                past = [history[rows, frame * FFT + column : frame * FFT + column + lanes] for frame in range(HISTORY)]
                filtered = []
                for frame in range(FRAME_BLOCK):
                    at = frame * FFT + column
                    past.append(voltages[rows, at : at + lanes].astype(jnp.float32))
                    value = weights[0] * past[0]
                    for offset in range(1, TAPS):
                        value = value + weights[offset] * past[offset]
                    filtered.append(value)
                    past = past[1:]
                for frame in range(HISTORY):
                    history[rows, frame * FFT + column : frame * FFT + column + lanes] = past[frame]
                pieces.append(filtered)
            for frame in range(FRAME_BLOCK):
                for (residue, _), target in zip(groups, folded):
                    value = pieces[0][frame]
                    if folds == 2:
                        value = value + pieces[1][frame] if residue == 0 else value - pieces[1][frame]
                    high = value.astype(jnp.bfloat16)
                    low = (value - high.astype(jnp.float32)).astype(jnp.bfloat16)
                    at = pl.ds(pl.multiple_of(frame * inputs_here + step * ROWS, ROWS), ROWS)
                    target[at, start : start + lanes] = high
                    target[at, part + start : part + start + lanes] = low
                    target[at, 2 * part + start : 2 * part + start + lanes] = high
        return carry

    lax.fori_loop(0, inputs_here // ROWS, filter_rows, 0)

    for (_, channels), transform, source in zip(groups, transforms, folded):
        per_channel = transform.shape[0] // len(channels)
        batch = max(1, min(FRAME_BLOCK, 256 // inputs_here)) if inputs_here >= lanes else 1
        for first in range(0, FRAME_BLOCK, batch):
            result = lax.dot_general(
                transform[...],
                source[first * inputs_here : (first + batch) * inputs_here, :],
                (((1,), (1,)), ((), ())),
                preferred_element_type=jnp.float32,
            )
            for frame in range(batch):
                turned[pl.ds(first + frame, transform.shape[0], stride=FRAME_BLOCK), :] = result[
                    :, frame * inputs_here : (frame + 1) * inputs_here
                ]
        for index, channel in enumerate(channels):
            start = index * per_channel * FRAME_BLOCK
            block = turned[start : start + per_channel * FRAME_BLOCK, :]
            chunk, slot = places[channel]
            block = block.reshape(per_channel // 2, 2, FRAME_BLOCK, inputs_here)
            outputs[chunk][:, slot] = block.astype(jnp.bfloat16)


def spectra(voltages, history, first_block, blocks, arrays, devices, chan_local):
    folds = 2 if chan_local % 2 == 0 else 1
    inputs_here = voltages.shape[0]
    places = {}
    groups = []
    for index, (channels, _, _, _, _) in enumerate(arrays):
        places.update({channel: (index, slot) for slot, channel in enumerate(channels)})
    for residue in range(folds):
        members = [channel for channel in sorted(places) if channel % folds == residue]
        if members:
            groups.append((residue, members))
    transforms = [jnp.asarray(build_transform(members, devices, chan_local, folds)) for _, members in groups]
    depth = 3 * (FFT // folds)
    most = max(transform.shape[0] for transform in transforms)
    existing = [(index, array[4]) for index, array in enumerate(arrays) if array[4] is not None]
    operand_count = 2 + len(history) + len(transforms)
    frames = blocks * FRAME_BLOCK
    return pl.pallas_call(
        functools.partial(spectra_kernel, groups, folds, places, len(history), len(arrays)),
        grid=(blocks,),
        in_specs=[pl.BlockSpec((inputs_here, FRAME_BLOCK * FFT), lambda step: (0, first_block + step))]
        + history_specs(history, inputs_here, first_block)
        + [pl.BlockSpec((TAPS, FFT), lambda step: (0, 0))]
        + [pl.BlockSpec(transform.shape, lambda step: (0, 0)) for transform in transforms]
        + [pl.BlockSpec(memory_space=pl.ANY) for _ in existing],
        out_specs=[
            pl.BlockSpec(
                (devices, len(channels), 2, FRAME_BLOCK, inputs_here),
                functools.partial(lambda at, step: (0, at, 0, step, 0), slot_block),
            )
            for channels, _, _, slot_block, _ in arrays
        ],
        out_shape=[
            jax.ShapeDtypeStruct((devices, slots, 2, array_frames, inputs_here), jnp.bfloat16)
            for _, slots, array_frames, _, _ in arrays
        ],
        input_output_aliases={operand_count + k: index for k, (index, _) in enumerate(existing)},
        scratch_shapes=[
            pltpu.VMEM((inputs_here, HISTORY * FFT), jnp.float32),
            pltpu.VMEM((most * FRAME_BLOCK, inputs_here), jnp.float32),
        ]
        + [pltpu.VMEM((FRAME_BLOCK * inputs_here, depth), jnp.bfloat16) for _ in groups],
        compiler_params=pltpu.CompilerParams(vmem_limit_bytes=VMEM_LIMIT),
        cost_estimate=pl.CostEstimate(
            flops=2 * frames * inputs_here * depth * sum(transform.shape[0] for transform in transforms),
            bytes_accessed=frames * inputs_here * (4 * FFT + 4 * devices * len(places)),
            transcendentals=0,
        ),
        name="spectra",
    )(
        voltages,
        *history,
        jnp.asarray(build_taps().astype(np.float32)),
        *transforms,
        *[array for _, array in existing],
    )


def visibility_kernel(piece_count, carried, *refs):
    pieces = refs[:piece_count]
    across, turned, swapped = refs[-3:]
    real_out, imag_out = refs[-5 - carried : -3 - carried][:2]
    depth = across.shape[0]
    total_frames = depth // 2
    row_block = real_out.shape[1]

    @pl.when(pl.program_id(1) == 0)
    def _():
        top = 0
        for piece in pieces:
            chan_count, blk_count, _, _, frames, inputs_here = piece.shape
            rows = blk_count * 2 * frames
            for chan in range(chan_count):
                columns = slice(chan * inputs_here, (chan + 1) * inputs_here)
                across[top : top + rows, columns] = piece[chan].reshape(rows, inputs_here)
            top += rows

    start = pl.multiple_of(pl.program_id(1) * row_block, row_block)
    turned[...] = across[:, pl.ds(start, row_block)].T
    top = 0
    for piece in pieces:
        frames = piece.shape[4]
        for at in range(top, top + piece.shape[1] * 2 * frames, 2 * frames):
            swapped[:, at : at + frames] = turned[:, at + frames : at + 2 * frames]
            swapped[:, at + frames : at + 2 * frames] = -turned[:, at : at + frames]
        top += piece.shape[1] * 2 * frames
    everything = across[...]
    real_out[0] = jnp.dot(turned[...], everything, preferred_element_type=jnp.float32) / total_frames
    imag_out[0] = jnp.dot(swapped[...], everything, preferred_element_type=jnp.float32) / total_frames


def visibilities(pieces, channels, before, carry, chan_local, in_vmem=False):
    arrays = [array for array, _ in pieces]
    chan_count, blk_count, _, _, _, inputs_here = arrays[0].shape
    inputs = chan_count * inputs_here
    depth = sum(blk_count * 2 * array.shape[4] for array in arrays)
    row_block = 256
    shape = jax.ShapeDtypeStruct((chan_local, inputs, inputs), jnp.float32)
    out_spec = pl.BlockSpec((1, row_block, inputs), lambda channel, step: (channels[0] + channel, step, 0))
    anywhere = pl.BlockSpec(memory_space=pl.ANY)
    aliases = {len(arrays) + index: index for index in range(len(before))}
    aliases.update({len(arrays) + len(before) + index: 2 + index for index in range(len(carry))})
    if in_vmem:
        piece_specs = [pl.BlockSpec(memory_space=pltpu.VMEM) for _ in arrays]
    else:
        piece_specs = [
            pl.BlockSpec(
                (chan_count, blk_count, 1, 2, array.shape[4], inputs_here),
                functools.partial(lambda slot, channel, step: (0, 0, slot + channel, 0, 0, 0), slot),
            )
            for array, slot in pieces
        ]
    results = pl.pallas_call(
        functools.partial(visibility_kernel, len(arrays), len(carry)),
        grid=(len(channels), inputs // row_block),
        in_specs=piece_specs + [anywhere for _ in before] + [anywhere for _ in carry],
        out_specs=[out_spec, out_spec] + [anywhere for _ in carry],
        out_shape=[shape, shape] + [jax.ShapeDtypeStruct(array.shape, array.dtype) for array in carry],
        input_output_aliases=aliases,
        scratch_shapes=[
            pltpu.VMEM((depth, inputs), jnp.bfloat16),
            pltpu.VMEM((row_block, depth), jnp.bfloat16),
            pltpu.VMEM((row_block, depth), jnp.bfloat16),
        ],
        compiler_params=pltpu.CompilerParams(vmem_limit_bytes=VISIBILITY_LIMIT),
        cost_estimate=pl.CostEstimate(
            flops=4 * len(channels) * inputs * inputs * depth,
            bytes_accessed=len(channels) * (2 * depth * inputs + 8 * inputs * inputs),
            transcendentals=0,
        ),
        name="visibilities",
    )(*arrays, *before, *carry)
    return tuple(results[:2]), list(results[2:])


def local(voltages):
    inputs_here = voltages.shape[0]
    frames_dev = voltages.shape[1] // FFT
    chan_count = lax.axis_size("chan")
    blk_count = lax.axis_size("blk")
    devices = chan_count * blk_count
    chan_local = NC // devices
    blocks = frames_dev // FRAME_BLOCK
    half = blocks // 2

    def exchange(array):
        arrived = lax.all_to_all(array, ("chan", "blk"), split_axis=0, concat_axis=0, tiled=True)
        return arrived.reshape(chan_count, blk_count, *array.shape[1:])

    if chan_local < 4 or chan_local % 2 or blocks % 2:
        tail = voltages[:, (frames_dev - HISTORY) * FFT :].astype(jnp.bfloat16)
        halo = shifted(tail, "blk", 1)
        outputs = ()
        arrays = [([channel], 1, frames_dev, 0, None) for channel in range(chan_local)]
        for channel, array in enumerate(spectra(voltages, [halo], 0, blocks, arrays, devices, chan_local)):
            outputs, _ = visibilities([(exchange(array), 0)], [channel], outputs, [], chan_local)
        return outputs

    first, second, last = 0, 2, 1
    rest = list(range(3, chan_local))
    early, tail = direct_spectra(voltages, first, half, devices, chan_local)
    halo = shifted(tail, "blk", 1)
    half_frames = half * FRAME_BLOCK
    (pair,) = spectra(
        voltages, [voltages] * HISTORY, half, half, [([second], 3, half_frames, 2, None)], devices, chan_local
    )
    (pair,) = spectra(voltages, [halo], 0, half, [([first, second], 3, half_frames, 0, pair)], devices, chan_local)
    many, final = spectra(
        voltages,
        [halo],
        0,
        blocks,
        [(rest, len(rest), frames_dev, 0, None), ([last], 1, frames_dev, 0, None)],
        devices,
        chan_local,
    )
    early = exchange(early)
    pair = exchange(pair)
    many = exchange(many)
    outputs, _ = visibilities([(early, 0), (pair, 0)], [first], (), [], chan_local)
    outputs, (final,) = visibilities([(pair, 1), (pair, 2)], [second], outputs, [final], chan_local)
    final = exchange(final)
    outputs, _ = visibilities([(many, 0)], rest, outputs, [], chan_local)
    outputs, _ = visibilities([(final, 0)], [last], outputs, [], chan_local, in_vmem=True)
    return outputs


def solution(mesh):
    return jax.shard_map(
        local,
        mesh=mesh,
        in_specs=(P("chan", "blk"),),
        out_specs=(P(("chan", "blk"), None, None), P(("chan", "blk"), None, None)),
        check_vma=False,
    )
```

```python
import functools

import jax
import jax.numpy as jnp
import numpy as np
from jax import lax
from jax.experimental import pallas as pl
from jax.experimental.pallas import tpu as pltpu
from jax.sharding import PartitionSpec as P

NC = 256
TAPS = 4
FFT = 512
HISTORY = TAPS - 1
FRAME_BLOCK = 16
ROWS = 16
VMEM_LIMIT = 56 * 1024 * 1024
VISIBILITY_LIMIT = 40 * 1024 * 1024


def shifted(value, axis, steps):
    count = lax.axis_size(axis)
    leading, last = (max(0, -steps), min(count, count - steps))
    return lax.ppermute(value, axis, [(source, source + steps) for source in range(leading, last)])


def build_taps():
    length = TAPS * FFT
    points = np.arange(length, dtype=np.float64)
    window = 0.54 - 0.46 * np.cos(2.0 * np.pi * points / (length - 1))
    return (np.sinc((points - (length - 1) / 2.0) / FFT) * window).reshape(TAPS, FFT)


def spectrum_scale(filter_taps):
    energy = np.mean(np.sum(filter_taps * filter_taps, axis=0))
    return 1.0 / (56.0 * np.sqrt(FFT * energy))


def build_dft(channels, devices, chan_local, points):
    rows = []
    for channel in channels:
        whole = np.arange(devices) * chan_local + channel
        angle = (whole[:, None] * np.arange(points)[None, :] % FFT) * (2.0 * np.pi / FFT)
        rows.append(np.stack([np.cos(angle), -np.sin(angle)], axis=1))
    return (np.concatenate(rows) * spectrum_scale(build_taps())).reshape(-1, points)


def split_high_low(matrix):
    matrix = matrix.astype(np.float32)
    high = matrix.astype(jnp.bfloat16)
    return high, (matrix - high.astype(np.float32)).astype(jnp.bfloat16)


def build_transform(channels, devices, chan_local, folds):
    high, low = split_high_low(build_dft(channels, devices, chan_local, FFT // folds))
    return np.concatenate([high, high, low], axis=1)


def build_direct(channel, devices, chan_local):
    matrix = build_dft([channel], devices, chan_local, FFT)
    high, low = split_high_low(np.concatenate([matrix * taps[None, :] for taps in build_taps()]))
    return np.concatenate([high, low], axis=0)


def history_specs(history, inputs_here, first_block):
    if len(history) == 1:
        return [pl.BlockSpec((inputs_here, HISTORY * FFT), lambda step: (0, 0))]
    before = first_block * FRAME_BLOCK - HISTORY
    return [pl.BlockSpec((inputs_here, FFT), functools.partial(lambda at, step: (0, at), before + k)) for k in range(HISTORY)]


def direct_kernel(history_count, voltages, *refs):
    history = refs[:history_count]
    transform, output, tail, products, turned = refs[history_count:]
    inputs_here = voltages.shape[0]
    rows = turned.shape[0] // FRAME_BLOCK
    batch = 2 if inputs_here == 128 else 1

    def multiply(target, frames):
        for first in range(0, len(frames), batch):
            group = [source[:, at : at + FFT] for source, at in frames[first : first + batch]]
            samples = jnp.concatenate(group, axis=0).astype(jnp.float32).astype(jnp.bfloat16)
            result = lax.dot_general(
                transform[...], samples, (((1,), (1,)), ((), ())), preferred_element_type=jnp.float32
            )
            for frame in range(len(group)):
                products[target + first + frame] = result[:, frame * inputs_here : (frame + 1) * inputs_here]

    @pl.when(pl.program_id(0) == 0)
    def _():
        multiply(0, [(source, 0) for source in history])

    multiply(HISTORY, [(voltages, frame * FFT) for frame in range(FRAME_BLOCK)])
    for frame in range(FRAME_BLOCK):
        total = None
        for part in (1, 0):
            for offset in range(TAPS):
                start = (part * TAPS + offset) * rows
                term = products[frame + offset, start : start + rows, :]
                total = term if total is None else total + term
        turned[pl.ds(frame, rows, stride=FRAME_BLOCK), :] = total
    for frame in range(HISTORY):
        products[frame] = products[FRAME_BLOCK + frame]
    output[...] = turned[...].reshape(output.shape).astype(jnp.bfloat16)

    @pl.when(pl.program_id(0) == pl.num_programs(0) - 1)
    def _():
        tail[...] = voltages[:, (FRAME_BLOCK - HISTORY) * FFT :].astype(jnp.float32).astype(jnp.bfloat16)


def direct_spectra(voltages, channel, first_block, devices, chan_local):
    inputs_here = voltages.shape[0]
    frames = voltages.shape[1] // FFT - first_block * FRAME_BLOCK
    transform = jnp.asarray(build_direct(channel, devices, chan_local))
    history = [voltages] * HISTORY
    return pl.pallas_call(
        functools.partial(direct_kernel, len(history)),
        grid=(frames // FRAME_BLOCK,),
        in_specs=[pl.BlockSpec((inputs_here, FRAME_BLOCK * FFT), lambda step: (0, first_block + step))]
        + history_specs(history, inputs_here, first_block)
        + [pl.BlockSpec(transform.shape, lambda step: (0, 0))],
        out_specs=[
            pl.BlockSpec((devices, 1, 2, FRAME_BLOCK, inputs_here), lambda step: (0, 0, 0, step, 0)),
            pl.BlockSpec((inputs_here, HISTORY * FFT), lambda step: (0, 0)),
        ],
        out_shape=[
            jax.ShapeDtypeStruct((devices, 1, 2, frames, inputs_here), jnp.bfloat16),
            jax.ShapeDtypeStruct((inputs_here, HISTORY * FFT), jnp.bfloat16),
        ],
        scratch_shapes=[
            pltpu.VMEM((HISTORY + FRAME_BLOCK, transform.shape[0], inputs_here), jnp.float32),
            pltpu.VMEM((devices * 2 * FRAME_BLOCK, inputs_here), jnp.float32),
        ],
        compiler_params=pltpu.CompilerParams(vmem_limit_bytes=VMEM_LIMIT),
        cost_estimate=pl.CostEstimate(
            flops=2 * frames * inputs_here * FFT * transform.shape[0],
            bytes_accessed=frames * inputs_here * (4 * FFT + 4 * devices),
            transcendentals=0,
        ),
        name="direct_spectra",
    )(voltages, *history, transform)


def spectra_kernel(groups, folds, places, history_count, array_count, voltages, *refs):
    before = refs[:history_count]
    taps = refs[history_count]
    transforms = refs[history_count + 1 : history_count + 1 + len(groups)]
    history, turned = refs[-2 - len(groups) : len(refs) - len(groups)]
    folded = refs[len(refs) - len(groups) :]
    outputs = refs[-2 - len(groups) - array_count : -2 - len(groups)]
    inputs_here = voltages.shape[0]
    part = FFT // folds
    lanes = 128

    @pl.when(pl.program_id(0) == 0)
    def _():
        at = 0
        for source in before:
            history[:, at : at + source.shape[1]] = source[...].astype(jnp.float32)
            at += source.shape[1]

    def filter_rows(step, carry):
        rows = pl.ds(pl.multiple_of(step * ROWS, ROWS), ROWS)
        for start in range(0, part, lanes):
            columns = [fold * part + start for fold in range(folds)]
            weights = [[taps[offset : offset + 1, at : at + lanes] for offset in range(TAPS)] for at in columns]
            past = [[history[rows, k * FFT + at : k * FFT + at + lanes] for k in range(HISTORY)] for at in columns]
            for frame in range(FRAME_BLOCK):
                filtered = []
                for fold, column in enumerate(columns):
                    at = frame * FFT + column
                    past[fold].append(voltages[rows, at : at + lanes].astype(jnp.float32))
                    value = weights[fold][0] * past[fold].pop(0)
                    for offset in range(1, TAPS):
                        value = value + weights[fold][offset] * past[fold][offset - 1]
                    filtered.append(value)
                for (residue, _), target in zip(groups, folded):
                    value = filtered[0]
                    if folds == 2:
                        value = value + filtered[1] if residue == 0 else value - filtered[1]
                    high = value.astype(jnp.bfloat16)
                    low = (value - high.astype(jnp.float32)).astype(jnp.bfloat16)
                    at = pl.ds(pl.multiple_of(frame * inputs_here + step * ROWS, ROWS), ROWS)
                    target[at, start : start + lanes] = high
                    target[at, part + start : part + start + lanes] = low
                    target[at, 2 * part + start : 2 * part + start + lanes] = high
            for fold, at in enumerate(columns):
                for k in range(HISTORY):
                    history[rows, k * FFT + at : k * FFT + at + lanes] = past[fold][k]
        return carry

    lax.fori_loop(0, inputs_here // ROWS, filter_rows, 0)

    for (_, channels), transform, source in zip(groups, transforms, folded):
        per_channel = transform.shape[0] // len(channels)
        batch = max(1, min(FRAME_BLOCK, 256 // inputs_here)) if inputs_here >= lanes else 1
        for first in range(0, FRAME_BLOCK, batch):
            result = lax.dot_general(
                transform[...],
                source[first * inputs_here : (first + batch) * inputs_here, :],
                (((1,), (1,)), ((), ())),
                preferred_element_type=jnp.float32,
            )
            for frame in range(batch):
                turned[pl.ds(first + frame, transform.shape[0], stride=FRAME_BLOCK), :] = result[
                    :, frame * inputs_here : (frame + 1) * inputs_here
                ]
        for index, channel in enumerate(channels):
            start = index * per_channel * FRAME_BLOCK
            block = turned[start : start + per_channel * FRAME_BLOCK, :]
            chunk, slot = places[channel]
            block = block.reshape(per_channel // 2, 2, FRAME_BLOCK, inputs_here)
            outputs[chunk][:, slot] = block.astype(jnp.bfloat16)


def spectra(voltages, history, first_block, blocks, arrays, devices, chan_local):
    folds = 2 if chan_local % 2 == 0 else 1
    inputs_here = voltages.shape[0]
    places = {}
    groups = []
    for index, (channels, _, _, _, _) in enumerate(arrays):
        places.update({channel: (index, slot) for slot, channel in enumerate(channels)})
    for residue in range(folds):
        members = [channel for channel in sorted(places) if channel % folds == residue]
        if members:
            groups.append((residue, members))
    transforms = [jnp.asarray(build_transform(members, devices, chan_local, folds)) for _, members in groups]
    depth = 3 * (FFT // folds)
    most = max(transform.shape[0] for transform in transforms)
    existing = [(index, array[4]) for index, array in enumerate(arrays) if array[4] is not None]
    operand_count = 2 + len(history) + len(transforms)
    frames = blocks * FRAME_BLOCK
    return pl.pallas_call(
        functools.partial(spectra_kernel, groups, folds, places, len(history), len(arrays)),
        grid=(blocks,),
        in_specs=[pl.BlockSpec((inputs_here, FRAME_BLOCK * FFT), lambda step: (0, first_block + step))]
        + history_specs(history, inputs_here, first_block)
        + [pl.BlockSpec((TAPS, FFT), lambda step: (0, 0))]
        + [pl.BlockSpec(transform.shape, lambda step: (0, 0)) for transform in transforms]
        + [pl.BlockSpec(memory_space=pl.ANY) for _ in existing],
        out_specs=[
            pl.BlockSpec(
                (devices, len(channels), 2, FRAME_BLOCK, inputs_here),
                place,
            )
            for channels, _, _, place, _ in arrays
        ],
        out_shape=[
            jax.ShapeDtypeStruct((devices, units, 2, unit_frames, inputs_here), jnp.bfloat16)
            for _, units, unit_frames, _, _ in arrays
        ],
        input_output_aliases={operand_count + k: index for k, (index, _) in enumerate(existing)},
        scratch_shapes=[
            pltpu.VMEM((inputs_here, HISTORY * FFT), jnp.float32),
            pltpu.VMEM((most * FRAME_BLOCK, inputs_here), jnp.float32),
        ]
        + [pltpu.VMEM((FRAME_BLOCK * inputs_here, depth), jnp.bfloat16) for _ in groups],
        compiler_params=pltpu.CompilerParams(vmem_limit_bytes=VMEM_LIMIT),
        cost_estimate=pl.CostEstimate(
            flops=2 * frames * inputs_here * depth * sum(transform.shape[0] for transform in transforms),
            bytes_accessed=frames * inputs_here * (4 * FFT + 4 * devices * len(places)),
            transcendentals=0,
        ),
        name="spectra",
    )(
        voltages,
        *history,
        jnp.asarray(build_taps().astype(np.float32)),
        *transforms,
        *[array for _, array in existing],
    )


def visibility_kernel(piece_units, carried, *refs):
    pieces = refs[: len(piece_units)]
    across, turned, swapped = refs[-3:]
    real_out, imag_out = refs[-5 - carried : -3 - carried][:2]
    total_frames = across.shape[0] // 2
    row_block = real_out.shape[1]

    @pl.when(pl.program_id(1) == 0)
    def _():
        top = 0
        for piece, units in zip(pieces, piece_units):
            chan_count, blk_count, _, _, frames, inputs_here = piece.shape
            for blk in range(blk_count):
                for unit in units:
                    for part in range(2):
                        rows = slice(part * total_frames + top, part * total_frames + top + frames)
                        for chan in range(chan_count):
                            columns = slice(chan * inputs_here, (chan + 1) * inputs_here)
                            across[rows, columns] = piece[chan, blk, unit, part]
                    top += frames

    start = pl.multiple_of(pl.program_id(1) * row_block, row_block)
    turned[...] = across[:, pl.ds(start, row_block)].T
    swapped[:, :total_frames] = turned[:, total_frames:]
    swapped[:, total_frames:] = -turned[:, :total_frames]
    everything = across[...]
    real_out[0] = jnp.dot(turned[...], everything, preferred_element_type=jnp.float32) / total_frames
    imag_out[0] = jnp.dot(swapped[...], everything, preferred_element_type=jnp.float32) / total_frames


def visibilities(pieces, channels, before, carry, chan_local, in_vmem=False):
    arrays = [array for array, _ in pieces]
    piece_units = [units or [0] for _, units in pieces]
    chan_count, blk_count, _, _, _, inputs_here = arrays[0].shape
    inputs = chan_count * inputs_here
    depth = sum(blk_count * 2 * array.shape[4] * len(units) for array, units in zip(arrays, piece_units))
    row_block = 256
    shape = jax.ShapeDtypeStruct((chan_local, inputs, inputs), jnp.float32)
    out_spec = pl.BlockSpec((1, row_block, inputs), lambda channel, step: (channels[0] + channel, step, 0))
    anywhere = pl.BlockSpec(memory_space=pl.ANY)
    aliases = {len(arrays) + index: index for index in range(len(before))}
    aliases.update({len(arrays) + len(before) + index: 2 + index for index in range(len(carry))})
    piece_specs = []
    for array, units in pieces:
        if in_vmem:
            piece_specs.append(pl.BlockSpec(memory_space=pltpu.VMEM))
        elif units:
            piece_specs.append(pl.BlockSpec(array.shape, lambda channel, step: (0, 0, 0, 0, 0, 0)))
        else:
            block = (chan_count, blk_count, 1) + array.shape[3:]
            piece_specs.append(pl.BlockSpec(block, lambda channel, step: (0, 0, channel, 0, 0, 0)))
    results = pl.pallas_call(
        functools.partial(visibility_kernel, piece_units, len(carry)),
        grid=(len(channels), inputs // row_block),
        in_specs=piece_specs + [anywhere for _ in before] + [anywhere for _ in carry],
        out_specs=[out_spec, out_spec] + [anywhere for _ in carry],
        out_shape=[shape, shape] + [jax.ShapeDtypeStruct(array.shape, array.dtype) for array in carry],
        input_output_aliases=aliases,
        scratch_shapes=[
            pltpu.VMEM((depth, inputs), jnp.bfloat16),
            pltpu.VMEM((row_block, depth), jnp.bfloat16),
            pltpu.VMEM((row_block, depth), jnp.bfloat16),
        ],
        compiler_params=pltpu.CompilerParams(vmem_limit_bytes=VISIBILITY_LIMIT),
        cost_estimate=pl.CostEstimate(
            flops=4 * len(channels) * inputs * inputs * depth,
            bytes_accessed=len(channels) * (2 * depth * inputs + 8 * inputs * inputs),
            transcendentals=0,
        ),
        name="visibilities",
    )(*arrays, *before, *carry)
    return tuple(results[:2]), list(results[2:])


def local(voltages):
    inputs_here = voltages.shape[0]
    frames_dev = voltages.shape[1] // FFT
    chan_count = lax.axis_size("chan")
    blk_count = lax.axis_size("blk")
    devices = chan_count * blk_count
    chan_local = NC // devices
    blocks = frames_dev // FRAME_BLOCK
    upper = blocks * 3 // 8
    lower = blocks - upper

    def exchange(array):
        arrived = lax.all_to_all(array, ("chan", "blk"), split_axis=0, concat_axis=0, tiled=True)
        return arrived.reshape(chan_count, blk_count, *array.shape[1:])

    def frame_by_frame(step):
        return (0, 0, 0, step, 0)

    def unit_by_unit(first, step):
        return (0, first + step, 0, 0, 0)

    if chan_local < 4 or chan_local % 2 or upper == 0:
        tail = voltages[:, (frames_dev - HISTORY) * FFT :].astype(jnp.bfloat16)
        halo = shifted(tail, "blk", 1)
        outputs = ()
        arrays = [([channel], 1, frames_dev, frame_by_frame, None) for channel in range(chan_local)]
        for channel, array in enumerate(spectra(voltages, [halo], 0, blocks, arrays, devices, chan_local)):
            outputs, _ = visibilities([(exchange(array), None)], [channel], outputs, [], chan_local)
        return outputs

    first, second, last = 0, 2, 1
    rest = list(range(3, chan_local))
    early, tail = direct_spectra(voltages, first, lower, devices, chan_local)
    halo = shifted(tail, "blk", 1)
    units = 2 * lower + upper
    above = functools.partial(unit_by_unit, 2 * lower)
    below = functools.partial(unit_by_unit, 0)
    (pair,) = spectra(
        voltages,
        [voltages] * HISTORY,
        lower,
        upper,
        [([second], units, FRAME_BLOCK, above, None)],
        devices,
        chan_local,
    )
    (pair,) = spectra(
        voltages, [halo], 0, lower, [([first, second], units, FRAME_BLOCK, below, pair)], devices, chan_local
    )
    many, final = spectra(
        voltages,
        [halo],
        0,
        blocks,
        [(rest, len(rest), frames_dev, frame_by_frame, None), ([last], 1, frames_dev, frame_by_frame, None)],
        devices,
        chan_local,
    )
    early = exchange(early)
    pair = exchange(pair)
    many = exchange(many)
    first_units = list(range(0, 2 * lower, 2))
    second_units = list(range(1, 2 * lower, 2)) + list(range(2 * lower, units))
    outputs, _ = visibilities([(early, [0]), (pair, first_units)], [first], (), [], chan_local)
    outputs, (final,) = visibilities([(pair, second_units)], [second], outputs, [final], chan_local)
    final = exchange(final)
    outputs, _ = visibilities([(many, None)], rest, outputs, [], chan_local)
    outputs, _ = visibilities([(final, None)], [last], outputs, [], chan_local, in_vmem=True)
    return outputs


def solution(mesh):
    return jax.shard_map(
        local,
        mesh=mesh,
        in_specs=(P("chan", "blk"),),
        out_specs=(P(("chan", "blk"), None, None), P(("chan", "blk"), None, None)),
        check_vma=False,
    )
```

```python
import functools

import jax
import jax.numpy as jnp
import numpy as np
from jax import lax
from jax.experimental import pallas as pl
from jax.experimental.pallas import tpu as pltpu
from jax.sharding import PartitionSpec as P

NC = 256
TAPS = 4
FFT = 512
HISTORY = TAPS - 1
FRAME_BLOCK = 16
ROWS = 16
VMEM_LIMIT = 56 * 1024 * 1024
VISIBILITY_LIMIT = 40 * 1024 * 1024


def shifted(value, axis, steps):
    count = lax.axis_size(axis)
    leading, last = (max(0, -steps), min(count, count - steps))
    return lax.ppermute(value, axis, [(source, source + steps) for source in range(leading, last)])


def build_taps():
    length = TAPS * FFT
    points = np.arange(length, dtype=np.float64)
    window = 0.54 - 0.46 * np.cos(2.0 * np.pi * points / (length - 1))
    return (np.sinc((points - (length - 1) / 2.0) / FFT) * window).reshape(TAPS, FFT)


def spectrum_scale(filter_taps):
    energy = np.mean(np.sum(filter_taps * filter_taps, axis=0))
    return 1.0 / (56.0 * np.sqrt(FFT * energy))


def build_dft(channels, devices, chan_local, points):
    rows = []
    for channel in channels:
        whole = np.arange(devices) * chan_local + channel
        angle = (whole[:, None] * np.arange(points)[None, :] % FFT) * (2.0 * np.pi / FFT)
        rows.append(np.stack([np.cos(angle), -np.sin(angle)], axis=1))
    return (np.concatenate(rows) * spectrum_scale(build_taps())).reshape(-1, points)


def split_high_low(matrix):
    matrix = matrix.astype(np.float32)
    high = matrix.astype(jnp.bfloat16)
    return high, (matrix - high.astype(np.float32)).astype(jnp.bfloat16)


def build_transform(channels, devices, chan_local, folds):
    high, low = split_high_low(build_dft(channels, devices, chan_local, FFT // folds))
    return np.concatenate([high, high, low], axis=1)


def build_direct(channel, devices, chan_local):
    matrix = build_dft([channel], devices, chan_local, FFT)
    high, low = split_high_low(np.concatenate([matrix * taps[None, :] for taps in build_taps()]))
    return np.concatenate([high, low], axis=0)


def history_specs(history, inputs_here, first_block):
    if len(history) == 1:
        return [pl.BlockSpec((inputs_here, HISTORY * FFT), lambda step: (0, 0))]
    before = first_block * FRAME_BLOCK - HISTORY
    return [pl.BlockSpec((inputs_here, FFT), functools.partial(lambda at, step: (0, at), before + k)) for k in range(HISTORY)]


def direct_kernel(history_count, voltages, *refs):
    history = refs[:history_count]
    transform, output, tail, products, turned = refs[history_count:]
    inputs_here = voltages.shape[0]
    rows = turned.shape[0] // FRAME_BLOCK
    batch = 2 if inputs_here == 128 else 1

    def multiply(target, frames):
        for first in range(0, len(frames), batch):
            group = [source[:, at : at + FFT] for source, at in frames[first : first + batch]]
            samples = jnp.concatenate(group, axis=0).astype(jnp.float32).astype(jnp.bfloat16)
            result = lax.dot_general(
                transform[...], samples, (((1,), (1,)), ((), ())), preferred_element_type=jnp.float32
            )
            for frame in range(len(group)):
                products[target + first + frame] = result[:, frame * inputs_here : (frame + 1) * inputs_here]

    @pl.when(pl.program_id(0) == 0)
    def _():
        multiply(0, [(source, 0) for source in history])

    multiply(HISTORY, [(voltages, frame * FFT) for frame in range(FRAME_BLOCK)])
    for frame in range(FRAME_BLOCK):
        total = None
        for part in (1, 0):
            for offset in range(TAPS):
                start = (part * TAPS + offset) * rows
                term = products[frame + offset, start : start + rows, :]
                total = term if total is None else total + term
        turned[pl.ds(frame, rows, stride=FRAME_BLOCK), :] = total
    for frame in range(HISTORY):
        products[frame] = products[FRAME_BLOCK + frame]
    output[...] = turned[...].reshape(output.shape).astype(jnp.bfloat16)

    @pl.when(pl.program_id(0) == pl.num_programs(0) - 1)
    def _():
        tail[...] = voltages[:, (FRAME_BLOCK - HISTORY) * FFT :].astype(jnp.float32).astype(jnp.bfloat16)


def direct_spectra(voltages, channel, first_block, units, unit_frames, place, devices, chan_local):
    inputs_here = voltages.shape[0]
    frames = voltages.shape[1] // FFT - first_block * FRAME_BLOCK
    transform = jnp.asarray(build_direct(channel, devices, chan_local))
    history = [voltages] * HISTORY
    return pl.pallas_call(
        functools.partial(direct_kernel, len(history)),
        grid=(frames // FRAME_BLOCK,),
        in_specs=[pl.BlockSpec((inputs_here, FRAME_BLOCK * FFT), lambda step: (0, first_block + step))]
        + history_specs(history, inputs_here, first_block)
        + [pl.BlockSpec(transform.shape, lambda step: (0, 0))],
        out_specs=[
            pl.BlockSpec((devices, 1, 2, FRAME_BLOCK, inputs_here), place),
            pl.BlockSpec((inputs_here, HISTORY * FFT), lambda step: (0, 0)),
        ],
        out_shape=[
            jax.ShapeDtypeStruct((devices, units, 2, unit_frames, inputs_here), jnp.bfloat16),
            jax.ShapeDtypeStruct((inputs_here, HISTORY * FFT), jnp.bfloat16),
        ],
        scratch_shapes=[
            pltpu.VMEM((HISTORY + FRAME_BLOCK, transform.shape[0], inputs_here), jnp.float32),
            pltpu.VMEM((devices * 2 * FRAME_BLOCK, inputs_here), jnp.float32),
        ],
        compiler_params=pltpu.CompilerParams(vmem_limit_bytes=VMEM_LIMIT),
        cost_estimate=pl.CostEstimate(
            flops=2 * frames * inputs_here * FFT * transform.shape[0],
            bytes_accessed=frames * inputs_here * (4 * FFT + 4 * devices),
            transcendentals=0,
        ),
        name="direct_spectra",
    )(voltages, *history, transform)


def spectra_kernel(groups, folds, places, history_count, array_count, voltages, *refs):
    before = refs[:history_count]
    taps = refs[history_count]
    transforms = refs[history_count + 1 : history_count + 1 + len(groups)]
    history, turned = refs[-2 - len(groups) : len(refs) - len(groups)]
    folded = refs[len(refs) - len(groups) :]
    outputs = refs[-2 - len(groups) - array_count : -2 - len(groups)]
    inputs_here = voltages.shape[0]
    part = FFT // folds
    lanes = 128

    @pl.when(pl.program_id(0) == 0)
    def _():
        at = 0
        for source in before:
            history[:, at : at + source.shape[1]] = source[...].astype(jnp.float32)
            at += source.shape[1]

    def filter_rows(step, carry):
        rows = pl.ds(pl.multiple_of(step * ROWS, ROWS), ROWS)
        for start in range(0, part, lanes):
            columns = [fold * part + start for fold in range(folds)]
            weights = [[taps[offset : offset + 1, at : at + lanes] for offset in range(TAPS)] for at in columns]
            past = [[history[rows, k * FFT + at : k * FFT + at + lanes] for k in range(HISTORY)] for at in columns]
            for frame in range(FRAME_BLOCK):
                filtered = []
                for fold, column in enumerate(columns):
                    at = frame * FFT + column
                    past[fold].append(voltages[rows, at : at + lanes].astype(jnp.float32))
                    value = weights[fold][0] * past[fold].pop(0)
                    for offset in range(1, TAPS):
                        value = value + weights[fold][offset] * past[fold][offset - 1]
                    filtered.append(value)
                for (residue, _), target in zip(groups, folded):
                    value = filtered[0]
                    if folds == 2:
                        value = value + filtered[1] if residue == 0 else value - filtered[1]
                    high = value.astype(jnp.bfloat16)
                    low = (value - high.astype(jnp.float32)).astype(jnp.bfloat16)
                    at = pl.ds(pl.multiple_of(frame * inputs_here + step * ROWS, ROWS), ROWS)
                    target[at, start : start + lanes] = high
                    target[at, part + start : part + start + lanes] = low
                    target[at, 2 * part + start : 2 * part + start + lanes] = high
            for fold, at in enumerate(columns):
                for k in range(HISTORY):
                    history[rows, k * FFT + at : k * FFT + at + lanes] = past[fold][k]
        return carry

    lax.fori_loop(0, inputs_here // ROWS, filter_rows, 0)

    for (_, channels), transform, source in zip(groups, transforms, folded):
        per_channel = transform.shape[0] // len(channels)
        batch = max(1, min(FRAME_BLOCK, 256 // inputs_here)) if inputs_here >= lanes else 1
        for first in range(0, FRAME_BLOCK, batch):
            result = lax.dot_general(
                transform[...],
                source[first * inputs_here : (first + batch) * inputs_here, :],
                (((1,), (1,)), ((), ())),
                preferred_element_type=jnp.float32,
            )
            for frame in range(batch):
                turned[pl.ds(first + frame, transform.shape[0], stride=FRAME_BLOCK), :] = result[
                    :, frame * inputs_here : (frame + 1) * inputs_here
                ]
        for index, channel in enumerate(channels):
            start = index * per_channel * FRAME_BLOCK
            block = turned[start : start + per_channel * FRAME_BLOCK, :]
            chunk, slot = places[channel]
            block = block.reshape(per_channel // 2, 2, FRAME_BLOCK, inputs_here)
            outputs[chunk][:, slot] = block.astype(jnp.bfloat16)


def spectra(voltages, history, first_block, blocks, arrays, devices, chan_local):
    folds = 2 if chan_local % 2 == 0 else 1
    inputs_here = voltages.shape[0]
    places = {}
    groups = []
    for index, (channels, _, _, _, _) in enumerate(arrays):
        places.update({channel: (index, slot) for slot, channel in enumerate(channels)})
    for residue in range(folds):
        members = [channel for channel in sorted(places) if channel % folds == residue]
        if members:
            groups.append((residue, members))
    transforms = [jnp.asarray(build_transform(members, devices, chan_local, folds)) for _, members in groups]
    depth = 3 * (FFT // folds)
    most = max(transform.shape[0] for transform in transforms)
    existing = [(index, array[4]) for index, array in enumerate(arrays) if array[4] is not None]
    operand_count = 2 + len(history) + len(transforms)
    frames = blocks * FRAME_BLOCK
    return pl.pallas_call(
        functools.partial(spectra_kernel, groups, folds, places, len(history), len(arrays)),
        grid=(blocks,),
        in_specs=[pl.BlockSpec((inputs_here, FRAME_BLOCK * FFT), lambda step: (0, first_block + step))]
        + history_specs(history, inputs_here, first_block)
        + [pl.BlockSpec((TAPS, FFT), lambda step: (0, 0))]
        + [pl.BlockSpec(transform.shape, lambda step: (0, 0)) for transform in transforms]
        + [pl.BlockSpec(memory_space=pl.ANY) for _ in existing],
        out_specs=[
            pl.BlockSpec(
                (devices, len(channels), 2, FRAME_BLOCK, inputs_here),
                place,
            )
            for channels, _, _, place, _ in arrays
        ],
        out_shape=[
            jax.ShapeDtypeStruct((devices, units, 2, unit_frames, inputs_here), jnp.bfloat16)
            for _, units, unit_frames, _, _ in arrays
        ],
        input_output_aliases={operand_count + k: index for k, (index, _) in enumerate(existing)},
        scratch_shapes=[
            pltpu.VMEM((inputs_here, HISTORY * FFT), jnp.float32),
            pltpu.VMEM((most * FRAME_BLOCK, inputs_here), jnp.float32),
        ]
        + [pltpu.VMEM((FRAME_BLOCK * inputs_here, depth), jnp.bfloat16) for _ in groups],
        compiler_params=pltpu.CompilerParams(vmem_limit_bytes=VMEM_LIMIT),
        cost_estimate=pl.CostEstimate(
            flops=2 * frames * inputs_here * depth * sum(transform.shape[0] for transform in transforms),
            bytes_accessed=frames * inputs_here * (4 * FFT + 4 * devices * len(places)),
            transcendentals=0,
        ),
        name="spectra",
    )(
        voltages,
        *history,
        jnp.asarray(build_taps().astype(np.float32)),
        *transforms,
        *[array for _, array in existing],
    )


def visibility_kernel(piece_units, carried, *refs):
    pieces = refs[: len(piece_units)]
    across, turned, swapped, above = refs[-4:]
    real_out, imag_out = refs[-6 - carried : -4 - carried][:2]
    total_frames = across.shape[0] // 2
    row_block, inputs = real_out.shape[1:]

    @pl.when(pl.program_id(1) == 0)
    def _():
        top = 0
        for piece, units in zip(pieces, piece_units):
            chan_count, blk_count, _, _, frames, inputs_here = piece.shape
            for blk in range(blk_count):
                for unit in units:
                    for part in range(2):
                        rows = slice(part * total_frames + top, part * total_frames + top + frames)
                        for chan in range(chan_count):
                            columns = slice(chan * inputs_here, (chan + 1) * inputs_here)
                            across[rows, columns] = piece[chan, blk, unit, part]
                    top += frames

    def one_block(step):
        start = step * row_block
        turned[...] = across[:, start : start + row_block].T
        swapped[:, :total_frames] = turned[:, total_frames:]
        swapped[:, total_frames:] = -turned[:, :total_frames]
        columns = across[:, start:]
        for index, (rows, output) in enumerate(((turned, real_out), (swapped, imag_out))):
            result = jnp.dot(rows[...], columns, preferred_element_type=jnp.float32) / total_frames
            output[0, :, start:] = result
            if start + row_block < inputs:
                above[index, start : start + row_block, start + row_block :] = result[:, row_block:]
            for left in range(0, start, row_block):
                mirrored = above[index, left : left + row_block, start : start + row_block].T
                output[0, :, left : left + row_block] = mirrored if index == 0 else -mirrored

    for step in range(inputs // row_block):
        pl.when(pl.program_id(1) == step)(functools.partial(one_block, step))


def visibilities(pieces, channels, before, carry, chan_local, in_vmem=False):
    arrays = [array for array, _ in pieces]
    piece_units = [units or [0] for _, units in pieces]
    chan_count, blk_count, _, _, _, inputs_here = arrays[0].shape
    inputs = chan_count * inputs_here
    depth = sum(blk_count * 2 * array.shape[4] * len(units) for array, units in zip(arrays, piece_units))
    row_block = 256
    shape = jax.ShapeDtypeStruct((chan_local, inputs, inputs), jnp.float32)
    out_spec = pl.BlockSpec((1, row_block, inputs), lambda channel, step: (channels[0] + channel, step, 0))
    anywhere = pl.BlockSpec(memory_space=pl.ANY)
    aliases = {len(arrays) + index: index for index in range(len(before))}
    aliases.update({len(arrays) + len(before) + index: 2 + index for index in range(len(carry))})
    piece_specs = []
    for array, units in pieces:
        if in_vmem:
            piece_specs.append(pl.BlockSpec(memory_space=pltpu.VMEM))
        elif units:
            piece_specs.append(pl.BlockSpec(array.shape, lambda channel, step: (0, 0, 0, 0, 0, 0)))
        else:
            block = (chan_count, blk_count, 1) + array.shape[3:]
            piece_specs.append(pl.BlockSpec(block, lambda channel, step: (0, 0, channel, 0, 0, 0)))
    results = pl.pallas_call(
        functools.partial(visibility_kernel, piece_units, len(carry)),
        grid=(len(channels), inputs // row_block),
        in_specs=piece_specs + [anywhere for _ in before] + [anywhere for _ in carry],
        out_specs=[out_spec, out_spec] + [anywhere for _ in carry],
        out_shape=[shape, shape] + [jax.ShapeDtypeStruct(array.shape, array.dtype) for array in carry],
        input_output_aliases=aliases,
        scratch_shapes=[
            pltpu.VMEM((depth, inputs), jnp.bfloat16),
            pltpu.VMEM((row_block, depth), jnp.bfloat16),
            pltpu.VMEM((row_block, depth), jnp.bfloat16),
            pltpu.VMEM((2, inputs, inputs), jnp.float32),
        ],
        compiler_params=pltpu.CompilerParams(vmem_limit_bytes=VISIBILITY_LIMIT),
        cost_estimate=pl.CostEstimate(
            flops=4 * len(channels) * inputs * inputs * depth,
            bytes_accessed=len(channels) * (2 * depth * inputs + 8 * inputs * inputs),
            transcendentals=0,
        ),
        name="visibilities",
    )(*arrays, *before, *carry)
    return tuple(results[:2]), list(results[2:])


def local(voltages):
    inputs_here = voltages.shape[0]
    frames_dev = voltages.shape[1] // FFT
    chan_count = lax.axis_size("chan")
    blk_count = lax.axis_size("blk")
    devices = chan_count * blk_count
    chan_local = NC // devices
    blocks = frames_dev // FRAME_BLOCK
    upper = blocks * 5 // 8
    lower = blocks - upper

    def exchange(array):
        arrived = lax.all_to_all(array, ("chan", "blk"), split_axis=0, concat_axis=0, tiled=True)
        return arrived.reshape(chan_count, blk_count, *array.shape[1:])

    def frame_by_frame(step):
        return (0, 0, 0, step, 0)

    def unit_by_unit(first, step):
        return (0, first + step, 0, 0, 0)

    if chan_local < 4 or chan_local % 2 or upper == 0:
        tail = voltages[:, (frames_dev - HISTORY) * FFT :].astype(jnp.bfloat16)
        halo = shifted(tail, "blk", 1)
        outputs = ()
        arrays = [([channel], 1, frames_dev, frame_by_frame, None) for channel in range(chan_local)]
        for channel, array in enumerate(spectra(voltages, [halo], 0, blocks, arrays, devices, chan_local)):
            outputs, _ = visibilities([(exchange(array), None)], [channel], outputs, [], chan_local)
        return outputs

    first, second, last = 0, 2, 1
    rest = list(range(3, chan_local))
    early, tail = direct_spectra(
        voltages, first, lower, 1, upper * FRAME_BLOCK, frame_by_frame, devices, chan_local
    )
    halo = shifted(tail, "blk", 1)
    units = 2 * lower + upper
    above = functools.partial(unit_by_unit, 2 * lower)
    below = functools.partial(unit_by_unit, 0)
    pair, _ = direct_spectra(voltages, second, lower, units, FRAME_BLOCK, above, devices, chan_local)
    (pair,) = spectra(
        voltages, [halo], 0, lower, [([first, second], units, FRAME_BLOCK, below, pair)], devices, chan_local
    )
    many, final = spectra(
        voltages,
        [halo],
        0,
        blocks,
        [(rest, len(rest), frames_dev, frame_by_frame, None), ([last], 1, frames_dev, frame_by_frame, None)],
        devices,
        chan_local,
    )
    early = exchange(early)
    pair = exchange(pair)
    many = exchange(many)
    first_units = list(range(0, 2 * lower, 2))
    second_units = list(range(1, 2 * lower, 2)) + list(range(2 * lower, units))
    outputs, _ = visibilities([(early, [0]), (pair, first_units)], [first], (), [], chan_local)
    outputs, (final,) = visibilities([(pair, second_units)], [second], outputs, [final], chan_local)
    final = exchange(final)
    outputs, _ = visibilities([(many, None)], rest, outputs, [], chan_local)
    outputs, _ = visibilities([(final, None)], [last], outputs, [], chan_local, in_vmem=True)
    return outputs


def solution(mesh):
    return jax.shard_map(
        local,
        mesh=mesh,
        in_specs=(P("chan", "blk"),),
        out_specs=(P(("chan", "blk"), None, None), P(("chan", "blk"), None, None)),
        check_vma=False,
    )
```

```python
import functools

import jax
import jax.numpy as jnp
import numpy as np
from jax import lax
from jax.experimental import pallas as pl
from jax.experimental.pallas import tpu as pltpu
from jax.sharding import PartitionSpec as P

NC = 256
TAPS = 4
FFT = 512
HISTORY = TAPS - 1
FRAME_BLOCK = 16
ROWS = 16
VMEM_LIMIT = 40 * 1024 * 1024
VISIBILITY_LIMIT = 40 * 1024 * 1024


def shifted(value, axis, steps):
    count = lax.axis_size(axis)
    leading, last = (max(0, -steps), min(count, count - steps))
    return lax.ppermute(value, axis, [(source, source + steps) for source in range(leading, last)])


def build_taps():
    length = TAPS * FFT
    points = np.arange(length, dtype=np.float64)
    window = 0.54 - 0.46 * np.cos(2.0 * np.pi * points / (length - 1))
    return (np.sinc((points - (length - 1) / 2.0) / FFT) * window).reshape(TAPS, FFT)


def spectrum_scale(filter_taps):
    energy = np.mean(np.sum(filter_taps * filter_taps, axis=0))
    return 1.0 / (56.0 * np.sqrt(FFT * energy))


def build_dft(channels, devices, chan_local, points):
    rows = []
    for channel in channels:
        whole = np.arange(devices) * chan_local + channel
        angle = (whole[:, None] * np.arange(points)[None, :] % FFT) * (2.0 * np.pi / FFT)
        rows.append(np.stack([np.cos(angle), -np.sin(angle)], axis=1))
    return (np.concatenate(rows) * spectrum_scale(build_taps())).reshape(-1, points)


def split_high_low(matrix):
    matrix = matrix.astype(np.float32)
    high = matrix.astype(jnp.bfloat16)
    return high, (matrix - high.astype(np.float32)).astype(jnp.bfloat16)


def build_transform(channels, devices, chan_local, folds):
    high, low = split_high_low(build_dft(channels, devices, chan_local, FFT // folds))
    return np.concatenate([high, high, low], axis=1)


def build_direct(channel, devices, chan_local):
    matrix = build_dft([channel], devices, chan_local, FFT)
    high, low = split_high_low(np.concatenate([matrix * taps[None, :] for taps in build_taps()]))
    return np.concatenate([high, low], axis=0)


def history_specs(history, inputs_here, first_block):
    if len(history) == 1:
        return [pl.BlockSpec((inputs_here, HISTORY * FFT), lambda step: (0, 0))]
    before = first_block * FRAME_BLOCK - HISTORY
    return [pl.BlockSpec((inputs_here, FFT), functools.partial(lambda at, step: (0, at), before + k)) for k in range(HISTORY)]


def direct_kernel(history_count, voltages, *refs):
    history = refs[:history_count]
    transform, output, tail, products, turned = refs[history_count:]
    inputs_here = voltages.shape[0]
    rows = turned.shape[0] // FRAME_BLOCK
    batch = 2 if inputs_here == 128 else 1

    newest = TAPS - 1

    def multiply(frames):
        samples = jnp.concatenate([source[:, at : at + FFT] for source, at in frames], axis=0)
        result = lax.dot_general(
            transform[...],
            samples.astype(jnp.float32).astype(jnp.bfloat16),
            (((1,), (1,)), ((), ())),
            preferred_element_type=jnp.float32,
        )
        return [result[:, k * inputs_here : (k + 1) * inputs_here] for k in range(len(frames))]

    def keep(place, product):
        for part in range(2):
            start = part * TAPS * rows
            kept = slice(part * newest * rows, (part + 1) * newest * rows)
            products[place, kept, :] = product[start : start + newest * rows]

    @pl.when(pl.program_id(0) == 0)
    def _():
        for k, source in enumerate(history):
            keep(k, multiply([(source, 0)])[0])

    for first in range(0, FRAME_BLOCK, batch):
        frames = range(first, first + batch)
        for frame, product in zip(frames, multiply([(voltages, frame * FFT) for frame in frames])):
            keep(HISTORY + frame, product)
            total = None
            for part in (1, 0):
                start = (part * TAPS + newest) * rows
                term = product[start : start + rows]
                total = term if total is None else total + term
                for offset in range(newest):
                    start = (part * newest + offset) * rows
                    total = total + products[frame + offset, start : start + rows, :]
            turned[pl.ds(frame, rows, stride=FRAME_BLOCK), :] = total
    for frame in range(HISTORY):
        products[frame] = products[FRAME_BLOCK + frame]
    output[...] = turned[...].reshape(output.shape).astype(jnp.bfloat16)

    @pl.when(pl.program_id(0) == pl.num_programs(0) - 1)
    def _():
        tail[...] = voltages[:, (FRAME_BLOCK - HISTORY) * FFT :].astype(jnp.float32).astype(jnp.bfloat16)


def direct_spectra(voltages, channel, first_block, units, unit_frames, place, devices, chan_local):
    inputs_here = voltages.shape[0]
    frames = voltages.shape[1] // FFT - first_block * FRAME_BLOCK
    transform = jnp.asarray(build_direct(channel, devices, chan_local))
    history = [voltages] * HISTORY
    return pl.pallas_call(
        functools.partial(direct_kernel, len(history)),
        grid=(frames // FRAME_BLOCK,),
        in_specs=[pl.BlockSpec((inputs_here, FRAME_BLOCK * FFT), lambda step: (0, first_block + step))]
        + history_specs(history, inputs_here, first_block)
        + [pl.BlockSpec(transform.shape, lambda step: (0, 0))],
        out_specs=[
            pl.BlockSpec((devices, 1, 2, FRAME_BLOCK, inputs_here), place),
            pl.BlockSpec((inputs_here, HISTORY * FFT), lambda step: (0, 0)),
        ],
        out_shape=[
            jax.ShapeDtypeStruct((devices, units, 2, unit_frames, inputs_here), jnp.bfloat16),
            jax.ShapeDtypeStruct((inputs_here, HISTORY * FFT), jnp.bfloat16),
        ],
        scratch_shapes=[
            pltpu.VMEM((HISTORY + FRAME_BLOCK, transform.shape[0] // TAPS * (TAPS - 1), inputs_here), jnp.float32),
            pltpu.VMEM((devices * 2 * FRAME_BLOCK, inputs_here), jnp.float32),
        ],
        compiler_params=pltpu.CompilerParams(vmem_limit_bytes=VMEM_LIMIT),
        cost_estimate=pl.CostEstimate(
            flops=2 * frames * inputs_here * FFT * transform.shape[0],
            bytes_accessed=frames * inputs_here * (4 * FFT + 4 * devices),
            transcendentals=0,
        ),
        name="direct_spectra",
    )(voltages, *history, transform)


def spectra_kernel(groups, folds, places, history_count, array_count, voltages, *refs):
    before = refs[:history_count]
    taps = refs[history_count]
    transforms = refs[history_count + 1 : history_count + 1 + len(groups)]
    history, turned = refs[-2 - len(groups) : len(refs) - len(groups)]
    folded = refs[len(refs) - len(groups) :]
    outputs = refs[-2 - len(groups) - array_count : -2 - len(groups)]
    inputs_here = voltages.shape[0]
    part = FFT // folds
    lanes = 128

    @pl.when(pl.program_id(0) == 0)
    def _():
        at = 0
        for source in before:
            history[:, at : at + source.shape[1]] = source[...].astype(jnp.float32)
            at += source.shape[1]

    def filter_rows(step, carry):
        rows = pl.ds(pl.multiple_of(step * ROWS, ROWS), ROWS)
        for start in range(0, part, lanes):
            columns = [fold * part + start for fold in range(folds)]
            weights = [[taps[offset : offset + 1, at : at + lanes] for offset in range(TAPS)] for at in columns]
            past = [[history[rows, k * FFT + at : k * FFT + at + lanes] for k in range(HISTORY)] for at in columns]
            for frame in range(FRAME_BLOCK):
                filtered = []
                for fold, column in enumerate(columns):
                    at = frame * FFT + column
                    past[fold].append(voltages[rows, at : at + lanes].astype(jnp.float32))
                    value = weights[fold][0] * past[fold].pop(0)
                    for offset in range(1, TAPS):
                        value = value + weights[fold][offset] * past[fold][offset - 1]
                    filtered.append(value)
                for (residue, _), target in zip(groups, folded):
                    value = filtered[0]
                    if folds == 2:
                        value = value + filtered[1] if residue == 0 else value - filtered[1]
                    high = value.astype(jnp.bfloat16)
                    low = (value - high.astype(jnp.float32)).astype(jnp.bfloat16)
                    at = pl.ds(pl.multiple_of(frame * inputs_here + step * ROWS, ROWS), ROWS)
                    target[at, start : start + lanes] = high
                    target[at, part + start : part + start + lanes] = low
                    target[at, 2 * part + start : 2 * part + start + lanes] = high
            for fold, at in enumerate(columns):
                for k in range(HISTORY):
                    history[rows, k * FFT + at : k * FFT + at + lanes] = past[fold][k]
        return carry

    lax.fori_loop(0, inputs_here // ROWS, filter_rows, 0)

    for (_, channels), transform, source in zip(groups, transforms, folded):
        per_channel = transform.shape[0] // len(channels)
        batch = max(1, min(FRAME_BLOCK, 256 // inputs_here)) if inputs_here >= lanes else 1
        for first in range(0, FRAME_BLOCK, batch):
            result = lax.dot_general(
                transform[...],
                source[first * inputs_here : (first + batch) * inputs_here, :],
                (((1,), (1,)), ((), ())),
                preferred_element_type=jnp.float32,
            )
            for frame in range(batch):
                turned[pl.ds(first + frame, transform.shape[0], stride=FRAME_BLOCK), :] = result[
                    :, frame * inputs_here : (frame + 1) * inputs_here
                ]
        for index, channel in enumerate(channels):
            start = index * per_channel * FRAME_BLOCK
            block = turned[start : start + per_channel * FRAME_BLOCK, :]
            chunk, slot = places[channel]
            block = block.reshape(per_channel // 2, 2, FRAME_BLOCK, inputs_here)
            outputs[chunk][:, slot] = block.astype(jnp.bfloat16)


def spectra(voltages, history, first_block, blocks, arrays, devices, chan_local):
    folds = 2 if chan_local % 2 == 0 else 1
    inputs_here = voltages.shape[0]
    places = {}
    groups = []
    for index, (channels, _, _, _, _) in enumerate(arrays):
        places.update({channel: (index, slot) for slot, channel in enumerate(channels)})
    for residue in range(folds):
        members = [channel for channel in sorted(places) if channel % folds == residue]
        if members:
            groups.append((residue, members))
    transforms = [jnp.asarray(build_transform(members, devices, chan_local, folds)) for _, members in groups]
    depth = 3 * (FFT // folds)
    most = max(transform.shape[0] for transform in transforms)
    existing = [(index, array[4]) for index, array in enumerate(arrays) if array[4] is not None]
    operand_count = 2 + len(history) + len(transforms)
    frames = blocks * FRAME_BLOCK
    return pl.pallas_call(
        functools.partial(spectra_kernel, groups, folds, places, len(history), len(arrays)),
        grid=(blocks,),
        in_specs=[pl.BlockSpec((inputs_here, FRAME_BLOCK * FFT), lambda step: (0, first_block + step))]
        + history_specs(history, inputs_here, first_block)
        + [pl.BlockSpec((TAPS, FFT), lambda step: (0, 0))]
        + [pl.BlockSpec(transform.shape, lambda step: (0, 0)) for transform in transforms]
        + [pl.BlockSpec(memory_space=pl.ANY) for _ in existing],
        out_specs=[
            pl.BlockSpec(
                (devices, len(channels), 2, FRAME_BLOCK, inputs_here),
                place,
            )
            for channels, _, _, place, _ in arrays
        ],
        out_shape=[
            jax.ShapeDtypeStruct((devices, units, 2, unit_frames, inputs_here), jnp.bfloat16)
            for _, units, unit_frames, _, _ in arrays
        ],
        input_output_aliases={operand_count + k: index for k, (index, _) in enumerate(existing)},
        scratch_shapes=[
            pltpu.VMEM((inputs_here, HISTORY * FFT), jnp.float32),
            pltpu.VMEM((most * FRAME_BLOCK, inputs_here), jnp.float32),
        ]
        + [pltpu.VMEM((FRAME_BLOCK * inputs_here, depth), jnp.bfloat16) for _ in groups],
        compiler_params=pltpu.CompilerParams(vmem_limit_bytes=VMEM_LIMIT),
        cost_estimate=pl.CostEstimate(
            flops=2 * frames * inputs_here * depth * sum(transform.shape[0] for transform in transforms),
            bytes_accessed=frames * inputs_here * (4 * FFT + 4 * devices * len(places)),
            transcendentals=0,
        ),
        name="spectra",
    )(
        voltages,
        *history,
        jnp.asarray(build_taps().astype(np.float32)),
        *transforms,
        *[array for _, array in existing],
    )


def visibility_kernel(piece_units, carried, *refs):
    pieces = refs[: len(piece_units)]
    across, turned, swapped, above = refs[-4:]
    real_out, imag_out = refs[-6 - carried : -4 - carried][:2]
    total_frames = across.shape[0] // 2
    row_block, inputs = real_out.shape[1:]

    @pl.when(pl.program_id(1) == 0)
    def _():
        top = 0
        for piece, units in zip(pieces, piece_units):
            chan_count, blk_count, _, _, frames, inputs_here = piece.shape
            for blk in range(blk_count):
                for unit in units:
                    for part in range(2):
                        rows = slice(part * total_frames + top, part * total_frames + top + frames)
                        for chan in range(chan_count):
                            columns = slice(chan * inputs_here, (chan + 1) * inputs_here)
                            across[rows, columns] = piece[chan, blk, unit, part]
                    top += frames

    def one_block(step):
        start = step * row_block
        turned[...] = across[:, start : start + row_block].T
        swapped[:, :total_frames] = turned[:, total_frames:]
        swapped[:, total_frames:] = -turned[:, :total_frames]
        columns = across[:, start:]
        for index, (rows, output) in enumerate(((turned, real_out), (swapped, imag_out))):
            result = jnp.dot(rows[...], columns, preferred_element_type=jnp.float32) / total_frames
            output[0, :, start:] = result
            if start + row_block < inputs:
                above[index, start : start + row_block, start + row_block :] = result[:, row_block:]
            for left in range(0, start, row_block):
                mirrored = above[index, left : left + row_block, start : start + row_block].T
                output[0, :, left : left + row_block] = mirrored if index == 0 else -mirrored

    for step in range(inputs // row_block):
        pl.when(pl.program_id(1) == step)(functools.partial(one_block, step))


def visibilities(pieces, channels, before, carry, chan_local, in_vmem=False):
    arrays = [array for array, _ in pieces]
    piece_units = [units or [0] for _, units in pieces]
    chan_count, blk_count, _, _, _, inputs_here = arrays[0].shape
    inputs = chan_count * inputs_here
    depth = sum(blk_count * 2 * array.shape[4] * len(units) for array, units in zip(arrays, piece_units))
    row_block = 256
    shape = jax.ShapeDtypeStruct((chan_local, inputs, inputs), jnp.float32)
    out_spec = pl.BlockSpec((1, row_block, inputs), lambda channel, step: (channels[0] + channel, step, 0))
    anywhere = pl.BlockSpec(memory_space=pl.ANY)
    aliases = {len(arrays) + index: index for index in range(len(before))}
    aliases.update({len(arrays) + len(before) + index: 2 + index for index in range(len(carry))})
    piece_specs = []
    for array, units in pieces:
        if in_vmem:
            piece_specs.append(pl.BlockSpec(memory_space=pltpu.VMEM))
        elif units:
            piece_specs.append(pl.BlockSpec(array.shape, lambda channel, step: (0, 0, 0, 0, 0, 0)))
        else:
            block = (chan_count, blk_count, 1) + array.shape[3:]
            piece_specs.append(pl.BlockSpec(block, lambda channel, step: (0, 0, channel, 0, 0, 0)))
    results = pl.pallas_call(
        functools.partial(visibility_kernel, piece_units, len(carry)),
        grid=(len(channels), inputs // row_block),
        in_specs=piece_specs + [anywhere for _ in before] + [anywhere for _ in carry],
        out_specs=[out_spec, out_spec] + [anywhere for _ in carry],
        out_shape=[shape, shape] + [jax.ShapeDtypeStruct(array.shape, array.dtype) for array in carry],
        input_output_aliases=aliases,
        scratch_shapes=[
            pltpu.VMEM((depth, inputs), jnp.bfloat16),
            pltpu.VMEM((row_block, depth), jnp.bfloat16),
            pltpu.VMEM((row_block, depth), jnp.bfloat16),
            pltpu.VMEM((2, inputs, inputs), jnp.float32),
        ],
        compiler_params=pltpu.CompilerParams(vmem_limit_bytes=VISIBILITY_LIMIT),
        cost_estimate=pl.CostEstimate(
            flops=4 * len(channels) * inputs * inputs * depth,
            bytes_accessed=len(channels) * (2 * depth * inputs + 8 * inputs * inputs),
            transcendentals=0,
        ),
        name="visibilities",
    )(*arrays, *before, *carry)
    return tuple(results[:2]), list(results[2:])


def local(voltages):
    inputs_here = voltages.shape[0]
    frames_dev = voltages.shape[1] // FFT
    chan_count = lax.axis_size("chan")
    blk_count = lax.axis_size("blk")
    devices = chan_count * blk_count
    chan_local = NC // devices
    blocks = frames_dev // FRAME_BLOCK
    upper = blocks * 5 // 8
    lower = blocks - upper

    def exchange(array):
        arrived = lax.all_to_all(array, ("chan", "blk"), split_axis=0, concat_axis=0, tiled=True)
        return arrived.reshape(chan_count, blk_count, *array.shape[1:])

    def frame_by_frame(step):
        return (0, 0, 0, step, 0)

    def unit_by_unit(first, step):
        return (0, first + step, 0, 0, 0)

    if chan_local < 4 or chan_local % 2 or upper == 0:
        tail = voltages[:, (frames_dev - HISTORY) * FFT :].astype(jnp.bfloat16)
        halo = shifted(tail, "blk", 1)
        outputs = ()
        arrays = [([channel], 1, frames_dev, frame_by_frame, None) for channel in range(chan_local)]
        for channel, array in enumerate(spectra(voltages, [halo], 0, blocks, arrays, devices, chan_local)):
            outputs, _ = visibilities([(exchange(array), None)], [channel], outputs, [], chan_local)
        return outputs

    first, second, last = 0, 2, 1
    rest = list(range(3, chan_local))
    early, tail = direct_spectra(
        voltages, first, lower, 1, upper * FRAME_BLOCK, frame_by_frame, devices, chan_local
    )
    halo = shifted(tail, "blk", 1)
    units = 2 * lower + upper
    above = functools.partial(unit_by_unit, 2 * lower)
    below = functools.partial(unit_by_unit, 0)
    pair, _ = direct_spectra(voltages, second, lower, units, FRAME_BLOCK, above, devices, chan_local)
    (pair,) = spectra(
        voltages, [halo], 0, lower, [([first, second], units, FRAME_BLOCK, below, pair)], devices, chan_local
    )
    many, final = spectra(
        voltages,
        [halo],
        0,
        blocks,
        [(rest, len(rest), frames_dev, frame_by_frame, None), ([last], 1, frames_dev, frame_by_frame, None)],
        devices,
        chan_local,
    )
    early = exchange(early)
    pair = exchange(pair)
    many = exchange(many)
    first_units = list(range(0, 2 * lower, 2))
    second_units = list(range(1, 2 * lower, 2)) + list(range(2 * lower, units))
    outputs, _ = visibilities([(early, [0]), (pair, first_units)], [first], (), [], chan_local)
    outputs, (final,) = visibilities([(pair, second_units)], [second], outputs, [final], chan_local)
    final = exchange(final)
    outputs, _ = visibilities([(many, None)], rest, outputs, [], chan_local)
    outputs, _ = visibilities([(final, None)], [last], outputs, [], chan_local, in_vmem=True)
    return outputs


def solution(mesh):
    return jax.shard_map(
        local,
        mesh=mesh,
        in_specs=(P("chan", "blk"),),
        out_specs=(P(("chan", "blk"), None, None), P(("chan", "blk"), None, None)),
        check_vma=False,
    )
```

```python
import functools

import jax
import jax.numpy as jnp
import numpy as np
from jax import lax
from jax.experimental import pallas as pl
from jax.experimental.pallas import tpu as pltpu
from jax.sharding import PartitionSpec as P

NC = 256
TAPS = 4
FFT = 512
HISTORY = TAPS - 1
FRAME_BLOCK = 16
ROWS = 16
VMEM_LIMIT = 56 * 1024 * 1024
VISIBILITY_LIMIT = 40 * 1024 * 1024


def shifted(value, axis, steps):
    count = lax.axis_size(axis)
    leading, last = (max(0, -steps), min(count, count - steps))
    return lax.ppermute(value, axis, [(source, source + steps) for source in range(leading, last)])


def build_taps():
    length = TAPS * FFT
    points = np.arange(length, dtype=np.float64)
    window = 0.54 - 0.46 * np.cos(2.0 * np.pi * points / (length - 1))
    return (np.sinc((points - (length - 1) / 2.0) / FFT) * window).reshape(TAPS, FFT)


def spectrum_scale(filter_taps):
    energy = np.mean(np.sum(filter_taps * filter_taps, axis=0))
    return 1.0 / (56.0 * np.sqrt(FFT * energy))


def build_dft(channels, devices, chan_local, points):
    rows = []
    for channel in channels:
        whole = np.arange(devices) * chan_local + channel
        angle = (whole[:, None] * np.arange(points)[None, :] % FFT) * (2.0 * np.pi / FFT)
        rows.append(np.stack([np.cos(angle), -np.sin(angle)], axis=1))
    return (np.concatenate(rows) * spectrum_scale(build_taps())).reshape(-1, points)


def split_high_low(matrix):
    matrix = matrix.astype(np.float32)
    high = matrix.astype(jnp.bfloat16)
    return high, (matrix - high.astype(np.float32)).astype(jnp.bfloat16)


def build_transform(channels, devices, chan_local, folds):
    high, low = split_high_low(build_dft(channels, devices, chan_local, FFT // folds))
    return np.concatenate([high, high, low], axis=1)


def build_direct(channel, devices, chan_local):
    matrix = build_dft([channel], devices, chan_local, FFT)
    high, low = split_high_low(np.concatenate([matrix * taps[None, :] for taps in build_taps()]))
    return np.concatenate([high, low], axis=0)


def row_groups(inputs_here):
    return 4 if inputs_here % (4 * ROWS) == 0 else 1


def sample_specs(inputs_here, first_block):
    count = row_groups(inputs_here)
    block = (inputs_here // count, FRAME_BLOCK * FFT)
    return [pl.BlockSpec(block, functools.partial(lambda at, step: (at, first_block + step), k)) for k in range(count)]


def history_specs(history, inputs_here, first_block):
    if len(history) == 1:
        return [pl.BlockSpec((inputs_here, HISTORY * FFT), lambda step: (0, 0))]
    before = first_block * FRAME_BLOCK - HISTORY
    return [pl.BlockSpec((inputs_here, FFT), functools.partial(lambda at, step: (0, at), before + k)) for k in range(HISTORY)]


def direct_kernel(group_count, history_count, *refs):
    voltages = refs[:group_count]
    history = refs[group_count : group_count + history_count]
    transform, output, tail, products, turned = refs[group_count + history_count :]
    inputs_here = tail.shape[0]
    rows = turned.shape[0] // FRAME_BLOCK
    batch = 2 if inputs_here == 128 else 1

    newest = TAPS - 1

    def multiply(frames):
        pieces = [source[:, at : at + FFT] for sources, at in frames for source in sources]
        samples = jnp.concatenate(pieces, axis=0)
        result = lax.dot_general(
            transform[...],
            samples.astype(jnp.float32).astype(jnp.bfloat16),
            (((1,), (1,)), ((), ())),
            preferred_element_type=jnp.float32,
        )
        return [result[:, k * inputs_here : (k + 1) * inputs_here] for k in range(len(frames))]

    def keep(place, product):
        for part in range(2):
            start = part * TAPS * rows
            kept = slice(part * newest * rows, (part + 1) * newest * rows)
            products[place, kept, :] = product[start : start + newest * rows]

    @pl.when(pl.program_id(0) == 0)
    def _():
        for k, source in enumerate(history):
            keep(k, multiply([([source], 0)])[0])

    for first in range(0, FRAME_BLOCK, batch):
        frames = range(first, first + batch)
        for frame, product in zip(frames, multiply([(voltages, frame * FFT) for frame in frames])):
            keep(HISTORY + frame, product)
            total = None
            for part in (1, 0):
                start = (part * TAPS + newest) * rows
                term = product[start : start + rows]
                total = term if total is None else total + term
                for offset in range(newest):
                    start = (part * newest + offset) * rows
                    total = total + products[frame + offset, start : start + rows, :]
            turned[pl.ds(frame, rows, stride=FRAME_BLOCK), :] = total
    for frame in range(HISTORY):
        products[frame] = products[FRAME_BLOCK + frame]
    output[...] = turned[...].reshape(output.shape).astype(jnp.bfloat16)

    @pl.when(pl.program_id(0) == pl.num_programs(0) - 1)
    def _():
        for k, source in enumerate(voltages):
            rows = slice(k * source.shape[0], (k + 1) * source.shape[0])
            tail[rows] = source[:, (FRAME_BLOCK - HISTORY) * FFT :].astype(jnp.float32).astype(jnp.bfloat16)


def direct_spectra(voltages, channel, first_block, units, unit_frames, place, devices, chan_local):
    inputs_here = voltages.shape[0]
    frames = voltages.shape[1] // FFT - first_block * FRAME_BLOCK
    transform = jnp.asarray(build_direct(channel, devices, chan_local))
    history = [voltages] * HISTORY
    return pl.pallas_call(
        functools.partial(direct_kernel, row_groups(inputs_here), len(history)),
        grid=(frames // FRAME_BLOCK,),
        in_specs=sample_specs(inputs_here, first_block)
        + history_specs(history, inputs_here, first_block)
        + [pl.BlockSpec(transform.shape, lambda step: (0, 0))],
        out_specs=[
            pl.BlockSpec((devices, 1, 2, FRAME_BLOCK, inputs_here), place),
            pl.BlockSpec((inputs_here, HISTORY * FFT), lambda step: (0, 0)),
        ],
        out_shape=[
            jax.ShapeDtypeStruct((devices, units, 2, unit_frames, inputs_here), jnp.bfloat16),
            jax.ShapeDtypeStruct((inputs_here, HISTORY * FFT), jnp.bfloat16),
        ],
        scratch_shapes=[
            pltpu.VMEM((HISTORY + FRAME_BLOCK, transform.shape[0] // TAPS * (TAPS - 1), inputs_here), jnp.float32),
            pltpu.VMEM((devices * 2 * FRAME_BLOCK, inputs_here), jnp.float32),
        ],
        compiler_params=pltpu.CompilerParams(vmem_limit_bytes=VMEM_LIMIT),
        cost_estimate=pl.CostEstimate(
            flops=2 * frames * inputs_here * FFT * transform.shape[0],
            bytes_accessed=frames * inputs_here * (4 * FFT + 4 * devices),
            transcendentals=0,
        ),
        name="direct_spectra",
    )(*[voltages] * row_groups(inputs_here), *history, transform)


def spectra_kernel(groups, folds, places, group_count, history_count, array_count, *refs):
    sources = refs[:group_count]
    refs = refs[group_count:]
    before = refs[:history_count]
    taps = refs[history_count]
    transforms = refs[history_count + 1 : history_count + 1 + len(groups)]
    history, turned = refs[-2 - len(groups) : len(refs) - len(groups)]
    folded = refs[len(refs) - len(groups) :]
    outputs = refs[-2 - len(groups) - array_count : -2 - len(groups)]
    inputs_here = history.shape[0]
    part = FFT // folds
    lanes = 128

    @pl.when(pl.program_id(0) == 0)
    def _():
        at = 0
        for source in before:
            history[:, at : at + source.shape[1]] = source[...].astype(jnp.float32)
            at += source.shape[1]

    def filter_rows(voltages, top, step, carry):
        here = pl.ds(pl.multiple_of(step * ROWS, ROWS), ROWS)
        rows = pl.ds(pl.multiple_of(top + step * ROWS, ROWS), ROWS)
        for start in range(0, part, lanes):
            columns = [fold * part + start for fold in range(folds)]
            weights = [[taps[offset : offset + 1, at : at + lanes] for offset in range(TAPS)] for at in columns]
            past = [[history[rows, k * FFT + at : k * FFT + at + lanes] for k in range(HISTORY)] for at in columns]
            for frame in range(FRAME_BLOCK):
                filtered = []
                for fold, column in enumerate(columns):
                    at = frame * FFT + column
                    past[fold].append(voltages[here, at : at + lanes].astype(jnp.float32))
                    value = weights[fold][0] * past[fold].pop(0)
                    for offset in range(1, TAPS):
                        value = value + weights[fold][offset] * past[fold][offset - 1]
                    filtered.append(value)
                for (residue, _), target in zip(groups, folded):
                    value = filtered[0]
                    if folds == 2:
                        value = value + filtered[1] if residue == 0 else value - filtered[1]
                    high = value.astype(jnp.bfloat16)
                    low = (value - high.astype(jnp.float32)).astype(jnp.bfloat16)
                    at = pl.ds(pl.multiple_of(frame * inputs_here + top + step * ROWS, ROWS), ROWS)
                    target[at, start : start + lanes] = high
                    target[at, part + start : part + start + lanes] = low
                    target[at, 2 * part + start : 2 * part + start + lanes] = high
            for fold, at in enumerate(columns):
                for k in range(HISTORY):
                    history[rows, k * FFT + at : k * FFT + at + lanes] = past[fold][k]
        return carry

    for index, source in enumerate(sources):
        height = source.shape[0]
        lax.fori_loop(0, height // ROWS, functools.partial(filter_rows, source, index * height), 0)

    for (_, channels), transform, source in zip(groups, transforms, folded):
        per_channel = transform.shape[0] // len(channels)
        batch = max(1, min(FRAME_BLOCK, 256 // inputs_here)) if inputs_here >= lanes else 1
        for first in range(0, FRAME_BLOCK, batch):
            result = lax.dot_general(
                transform[...],
                source[first * inputs_here : (first + batch) * inputs_here, :],
                (((1,), (1,)), ((), ())),
                preferred_element_type=jnp.float32,
            )
            for frame in range(batch):
                turned[pl.ds(first + frame, transform.shape[0], stride=FRAME_BLOCK), :] = result[
                    :, frame * inputs_here : (frame + 1) * inputs_here
                ]
        for index, channel in enumerate(channels):
            start = index * per_channel * FRAME_BLOCK
            block = turned[start : start + per_channel * FRAME_BLOCK, :]
            chunk, slot = places[channel]
            block = block.reshape(per_channel // 2, 2, FRAME_BLOCK, inputs_here)
            outputs[chunk][:, slot] = block.astype(jnp.bfloat16)


def spectra(voltages, history, first_block, blocks, arrays, devices, chan_local):
    folds = 2 if chan_local % 2 == 0 else 1
    inputs_here = voltages.shape[0]
    places = {}
    groups = []
    for index, (channels, _, _, _, _) in enumerate(arrays):
        places.update({channel: (index, slot) for slot, channel in enumerate(channels)})
    for residue in range(folds):
        members = [channel for channel in sorted(places) if channel % folds == residue]
        if members:
            groups.append((residue, members))
    transforms = [jnp.asarray(build_transform(members, devices, chan_local, folds)) for _, members in groups]
    depth = 3 * (FFT // folds)
    most = max(transform.shape[0] for transform in transforms)
    existing = [(index, array[4]) for index, array in enumerate(arrays) if array[4] is not None]
    operand_count = 1 + row_groups(inputs_here) + len(history) + len(transforms)
    frames = blocks * FRAME_BLOCK
    return pl.pallas_call(
        functools.partial(
            spectra_kernel, groups, folds, places, row_groups(inputs_here), len(history), len(arrays)
        ),
        grid=(blocks,),
        in_specs=sample_specs(inputs_here, first_block)
        + history_specs(history, inputs_here, first_block)
        + [pl.BlockSpec((TAPS, FFT), lambda step: (0, 0))]
        + [pl.BlockSpec(transform.shape, lambda step: (0, 0)) for transform in transforms]
        + [pl.BlockSpec(memory_space=pl.ANY) for _ in existing],
        out_specs=[
            pl.BlockSpec(
                (devices, len(channels), 2, FRAME_BLOCK, inputs_here),
                place,
            )
            for channels, _, _, place, _ in arrays
        ],
        out_shape=[
            jax.ShapeDtypeStruct((devices, units, 2, unit_frames, inputs_here), jnp.bfloat16)
            for _, units, unit_frames, _, _ in arrays
        ],
        input_output_aliases={operand_count + k: index for k, (index, _) in enumerate(existing)},
        scratch_shapes=[
            pltpu.VMEM((inputs_here, HISTORY * FFT), jnp.float32),
            pltpu.VMEM((most * FRAME_BLOCK, inputs_here), jnp.float32),
        ]
        + [pltpu.VMEM((FRAME_BLOCK * inputs_here, depth), jnp.bfloat16) for _ in groups],
        compiler_params=pltpu.CompilerParams(vmem_limit_bytes=VMEM_LIMIT),
        cost_estimate=pl.CostEstimate(
            flops=2 * frames * inputs_here * depth * sum(transform.shape[0] for transform in transforms),
            bytes_accessed=frames * inputs_here * (4 * FFT + 4 * devices * len(places)),
            transcendentals=0,
        ),
        name="spectra",
    )(
        *[voltages] * row_groups(inputs_here),
        *history,
        jnp.asarray(build_taps().astype(np.float32)),
        *transforms,
        *[array for _, array in existing],
    )


def visibility_kernel(piece_units, carried, *refs):
    pieces = refs[: len(piece_units)]
    across, turned, swapped, above = refs[-4:]
    real_out, imag_out = refs[-6 - carried : -4 - carried][:2]
    total_frames = across.shape[0] // 2
    row_block, inputs = real_out.shape[1:]

    @pl.when(pl.program_id(1) == 0)
    def _():
        top = 0
        for piece, units in zip(pieces, piece_units):
            chan_count, blk_count, _, _, frames, inputs_here = piece.shape
            for blk in range(blk_count):
                for unit in units:
                    for part in range(2):
                        rows = slice(part * total_frames + top, part * total_frames + top + frames)
                        for chan in range(chan_count):
                            columns = slice(chan * inputs_here, (chan + 1) * inputs_here)
                            across[rows, columns] = piece[chan, blk, unit, part]
                    top += frames

    def one_block(step):
        start = step * row_block
        turned[...] = across[:, start : start + row_block].T
        swapped[:, :total_frames] = turned[:, total_frames:]
        swapped[:, total_frames:] = -turned[:, :total_frames]
        columns = across[:, start:]
        for index, (rows, output) in enumerate(((turned, real_out), (swapped, imag_out))):
            result = jnp.dot(rows[...], columns, preferred_element_type=jnp.float32) / total_frames
            output[0, :, start:] = result
            if start + row_block < inputs:
                above[index, start : start + row_block, start + row_block :] = result[:, row_block:]
            for left in range(0, start, row_block):
                mirrored = above[index, left : left + row_block, start : start + row_block].T
                output[0, :, left : left + row_block] = mirrored if index == 0 else -mirrored

    for step in range(inputs // row_block):
        pl.when(pl.program_id(1) == step)(functools.partial(one_block, step))


def visibilities(pieces, channels, before, carry, chan_local, in_vmem=False):
    arrays = [array for array, _ in pieces]
    piece_units = [units or [0] for _, units in pieces]
    chan_count, blk_count, _, _, _, inputs_here = arrays[0].shape
    inputs = chan_count * inputs_here
    depth = sum(blk_count * 2 * array.shape[4] * len(units) for array, units in zip(arrays, piece_units))
    row_block = 256
    shape = jax.ShapeDtypeStruct((chan_local, inputs, inputs), jnp.float32)
    out_spec = pl.BlockSpec((1, row_block, inputs), lambda channel, step: (channels[0] + channel, step, 0))
    anywhere = pl.BlockSpec(memory_space=pl.ANY)
    aliases = {len(arrays) + index: index for index in range(len(before))}
    aliases.update({len(arrays) + len(before) + index: 2 + index for index in range(len(carry))})
    piece_specs = []
    for array, units in pieces:
        if in_vmem:
            piece_specs.append(pl.BlockSpec(memory_space=pltpu.VMEM))
        elif units:
            piece_specs.append(pl.BlockSpec(array.shape, lambda channel, step: (0, 0, 0, 0, 0, 0)))
        else:
            block = (chan_count, blk_count, 1) + array.shape[3:]
            piece_specs.append(pl.BlockSpec(block, lambda channel, step: (0, 0, channel, 0, 0, 0)))
    results = pl.pallas_call(
        functools.partial(visibility_kernel, piece_units, len(carry)),
        grid=(len(channels), inputs // row_block),
        in_specs=piece_specs + [anywhere for _ in before] + [anywhere for _ in carry],
        out_specs=[out_spec, out_spec] + [anywhere for _ in carry],
        out_shape=[shape, shape] + [jax.ShapeDtypeStruct(array.shape, array.dtype) for array in carry],
        input_output_aliases=aliases,
        scratch_shapes=[
            pltpu.VMEM((depth, inputs), jnp.bfloat16),
            pltpu.VMEM((row_block, depth), jnp.bfloat16),
            pltpu.VMEM((row_block, depth), jnp.bfloat16),
            pltpu.VMEM((2, inputs, inputs), jnp.float32),
        ],
        compiler_params=pltpu.CompilerParams(vmem_limit_bytes=VISIBILITY_LIMIT),
        cost_estimate=pl.CostEstimate(
            flops=4 * len(channels) * inputs * inputs * depth,
            bytes_accessed=len(channels) * (2 * depth * inputs + 8 * inputs * inputs),
            transcendentals=0,
        ),
        name="visibilities",
    )(*arrays, *before, *carry)
    return tuple(results[:2]), list(results[2:])


def local(voltages):
    inputs_here = voltages.shape[0]
    frames_dev = voltages.shape[1] // FFT
    chan_count = lax.axis_size("chan")
    blk_count = lax.axis_size("blk")
    devices = chan_count * blk_count
    chan_local = NC // devices
    blocks = frames_dev // FRAME_BLOCK
    upper = blocks * 5 // 8
    lower = blocks - upper

    def exchange(array):
        arrived = lax.all_to_all(array, ("chan", "blk"), split_axis=0, concat_axis=0, tiled=True)
        return arrived.reshape(chan_count, blk_count, *array.shape[1:])

    def frame_by_frame(step):
        return (0, 0, 0, step, 0)

    def unit_by_unit(first, step):
        return (0, first + step, 0, 0, 0)

    if chan_local < 4 or chan_local % 2 or upper == 0:
        tail = voltages[:, (frames_dev - HISTORY) * FFT :].astype(jnp.bfloat16)
        halo = shifted(tail, "blk", 1)
        outputs = ()
        arrays = [([channel], 1, frames_dev, frame_by_frame, None) for channel in range(chan_local)]
        for channel, array in enumerate(spectra(voltages, [halo], 0, blocks, arrays, devices, chan_local)):
            outputs, _ = visibilities([(exchange(array), None)], [channel], outputs, [], chan_local)
        return outputs

    first, second, last = 0, 2, 1
    rest = list(range(3, chan_local))
    early, tail = direct_spectra(
        voltages, first, lower, 1, upper * FRAME_BLOCK, frame_by_frame, devices, chan_local
    )
    halo = shifted(tail, "blk", 1)
    units = 2 * lower + upper
    above = functools.partial(unit_by_unit, 2 * lower)
    below = functools.partial(unit_by_unit, 0)
    pair, _ = direct_spectra(voltages, second, lower, units, FRAME_BLOCK, above, devices, chan_local)
    (pair,) = spectra(
        voltages, [halo], 0, lower, [([first, second], units, FRAME_BLOCK, below, pair)], devices, chan_local
    )
    many, final = spectra(
        voltages,
        [halo],
        0,
        blocks,
        [(rest, len(rest), frames_dev, frame_by_frame, None), ([last], 1, frames_dev, frame_by_frame, None)],
        devices,
        chan_local,
    )
    early = exchange(early)
    pair = exchange(pair)
    many = exchange(many)
    first_units = list(range(0, 2 * lower, 2))
    second_units = list(range(1, 2 * lower, 2)) + list(range(2 * lower, units))
    outputs, _ = visibilities([(early, [0]), (pair, first_units)], [first], (), [], chan_local)
    outputs, (final,) = visibilities([(pair, second_units)], [second], outputs, [final], chan_local)
    final = exchange(final)
    outputs, _ = visibilities([(many, None)], rest, outputs, [], chan_local)
    outputs, _ = visibilities([(final, None)], [last], outputs, [], chan_local, in_vmem=True)
    return outputs


def solution(mesh):
    return jax.shard_map(
        local,
        mesh=mesh,
        in_specs=(P("chan", "blk"),),
        out_specs=(P(("chan", "blk"), None, None), P(("chan", "blk"), None, None)),
        check_vma=False,
    )
```

```python
import functools

import jax
import jax.numpy as jnp
import numpy as np
from jax import lax
from jax.experimental import pallas as pl
from jax.experimental.pallas import tpu as pltpu
from jax.sharding import PartitionSpec as P

NC = 256
TAPS = 4
FFT = 512
HISTORY = TAPS - 1
FRAME_BLOCK = 16
ROWS = 16
VMEM_LIMIT = 56 * 1024 * 1024
VISIBILITY_LIMIT = 40 * 1024 * 1024


def shifted(value, axis, steps):
    count = lax.axis_size(axis)
    leading, last = (max(0, -steps), min(count, count - steps))
    return lax.ppermute(value, axis, [(source, source + steps) for source in range(leading, last)])


def build_taps():
    length = TAPS * FFT
    points = np.arange(length, dtype=np.float64)
    window = 0.54 - 0.46 * np.cos(2.0 * np.pi * points / (length - 1))
    return (np.sinc((points - (length - 1) / 2.0) / FFT) * window).reshape(TAPS, FFT)


def spectrum_scale(filter_taps):
    energy = np.mean(np.sum(filter_taps * filter_taps, axis=0))
    return 1.0 / (56.0 * np.sqrt(FFT * energy))


def build_dft(channels, devices, chan_local, points):
    rows = []
    for channel in channels:
        whole = np.arange(devices) * chan_local + channel
        angle = (whole[:, None] * np.arange(points)[None, :] % FFT) * (2.0 * np.pi / FFT)
        rows.append(np.stack([np.cos(angle), -np.sin(angle)], axis=1))
    return (np.concatenate(rows) * spectrum_scale(build_taps())).reshape(-1, points)


def split_high_low(matrix):
    matrix = matrix.astype(np.float32)
    high = matrix.astype(jnp.bfloat16)
    return high, (matrix - high.astype(np.float32)).astype(jnp.bfloat16)


def build_transform(channels, devices, chan_local, folds):
    high, low = split_high_low(build_dft(channels, devices, chan_local, FFT // folds))
    return np.concatenate([high, high, low], axis=1)


def build_direct(channel, devices, chan_local):
    matrix = build_dft([channel], devices, chan_local, FFT)
    parts = [part for taps in build_taps() for part in split_high_low(matrix * taps[None, :])]
    return np.ascontiguousarray(np.concatenate(parts, axis=0).T)


def history_specs(history, inputs_here, first_block):
    if len(history) == 1:
        return [pl.BlockSpec((inputs_here, HISTORY * FFT), lambda step: (0, 0))]
    before = first_block * FRAME_BLOCK - HISTORY
    return [pl.BlockSpec((inputs_here, FFT), functools.partial(lambda at, step: (0, at), before + k)) for k in range(HISTORY)]


def direct_kernel(history_count, voltages, *refs):
    history = refs[:history_count]
    transform, output, tail, products, turned = refs[history_count:]
    inputs_here = voltages.shape[0]
    rows = turned.shape[0] // FRAME_BLOCK
    batch = 2 if inputs_here == 128 else 1

    newest = TAPS - 1

    def multiply(frames):
        samples = jnp.concatenate([source[:, at : at + FFT] for source, at in frames], axis=0)
        samples = samples.astype(jnp.float32).astype(jnp.bfloat16)
        result = jnp.dot(samples, transform[...], preferred_element_type=jnp.float32)
        return [result[k * inputs_here : (k + 1) * inputs_here] for k in range(len(frames))]

    @pl.when(pl.program_id(0) == 0)
    def _():
        for k, source in enumerate(history):
            products[k] = multiply([(source, 0)])[0][:, : 2 * newest * rows]

    for first in range(0, FRAME_BLOCK, batch):
        frames = range(first, first + batch)
        for frame, product in zip(frames, multiply([(voltages, frame * FFT) for frame in frames])):
            products[HISTORY + frame] = product[:, : 2 * newest * rows]
            total = product[:, 2 * newest * rows :]
            for offset in range(newest):
                total = total + products[frame + offset, :, 2 * offset * rows : 2 * (offset + 1) * rows]
            total = total.T
            turned[pl.ds(frame, rows, stride=FRAME_BLOCK), :] = total[:rows] + total[rows:]
    for frame in range(HISTORY):
        products[frame] = products[FRAME_BLOCK + frame]
    output[...] = turned[...].reshape(output.shape).astype(jnp.bfloat16)

    @pl.when(pl.program_id(0) == pl.num_programs(0) - 1)
    def _():
        tail[...] = voltages[:, (FRAME_BLOCK - HISTORY) * FFT :].astype(jnp.float32).astype(jnp.bfloat16)


def direct_spectra(voltages, channel, first_block, units, unit_frames, place, devices, chan_local):
    inputs_here = voltages.shape[0]
    frames = voltages.shape[1] // FFT - first_block * FRAME_BLOCK
    transform = jnp.asarray(build_direct(channel, devices, chan_local))
    history = [voltages] * HISTORY
    return pl.pallas_call(
        functools.partial(direct_kernel, len(history)),
        grid=(frames // FRAME_BLOCK,),
        in_specs=[pl.BlockSpec((inputs_here, FRAME_BLOCK * FFT), lambda step: (0, first_block + step))]
        + history_specs(history, inputs_here, first_block)
        + [pl.BlockSpec(transform.shape, lambda step: (0, 0))],
        out_specs=[
            pl.BlockSpec((devices, 1, 2, FRAME_BLOCK, inputs_here), place),
            pl.BlockSpec((inputs_here, HISTORY * FFT), lambda step: (0, 0)),
        ],
        out_shape=[
            jax.ShapeDtypeStruct((devices, units, 2, unit_frames, inputs_here), jnp.bfloat16),
            jax.ShapeDtypeStruct((inputs_here, HISTORY * FFT), jnp.bfloat16),
        ],
        scratch_shapes=[
            pltpu.VMEM((HISTORY + FRAME_BLOCK, inputs_here, transform.shape[1] // TAPS * (TAPS - 1)), jnp.float32),
            pltpu.VMEM((devices * 2 * FRAME_BLOCK, inputs_here), jnp.float32),
        ],
        compiler_params=pltpu.CompilerParams(vmem_limit_bytes=VMEM_LIMIT),
        cost_estimate=pl.CostEstimate(
            flops=2 * frames * inputs_here * FFT * transform.shape[1],
            bytes_accessed=frames * inputs_here * (4 * FFT + 4 * devices),
            transcendentals=0,
        ),
        name="direct_spectra",
    )(voltages, *history, transform)


def spectra_kernel(groups, folds, places, history_count, array_count, voltages, *refs):
    before = refs[:history_count]
    taps = refs[history_count]
    transforms = refs[history_count + 1 : history_count + 1 + len(groups)]
    history, turned = refs[-2 - len(groups) : len(refs) - len(groups)]
    folded = refs[len(refs) - len(groups) :]
    outputs = refs[-2 - len(groups) - array_count : -2 - len(groups)]
    inputs_here = voltages.shape[0]
    part = FFT // folds
    lanes = 128

    @pl.when(pl.program_id(0) == 0)
    def _():
        at = 0
        for source in before:
            history[:, at : at + source.shape[1]] = source[...].astype(jnp.float32)
            at += source.shape[1]

    def filter_rows(step, carry):
        rows = pl.ds(pl.multiple_of(step * ROWS, ROWS), ROWS)
        for start in range(0, part, lanes):
            columns = [fold * part + start for fold in range(folds)]
            weights = [[taps[offset : offset + 1, at : at + lanes] for offset in range(TAPS)] for at in columns]
            past = [[history[rows, k * FFT + at : k * FFT + at + lanes] for k in range(HISTORY)] for at in columns]
            for frame in range(FRAME_BLOCK):
                filtered = []
                for fold, column in enumerate(columns):
                    at = frame * FFT + column
                    past[fold].append(voltages[rows, at : at + lanes].astype(jnp.float32))
                    value = weights[fold][0] * past[fold].pop(0)
                    for offset in range(1, TAPS):
                        value = value + weights[fold][offset] * past[fold][offset - 1]
                    filtered.append(value)
                for (residue, _), target in zip(groups, folded):
                    value = filtered[0]
                    if folds == 2:
                        value = value + filtered[1] if residue == 0 else value - filtered[1]
                    high = value.astype(jnp.bfloat16)
                    low = (value - high.astype(jnp.float32)).astype(jnp.bfloat16)
                    at = pl.ds(pl.multiple_of(frame * inputs_here + step * ROWS, ROWS), ROWS)
                    target[at, start : start + lanes] = high
                    target[at, part + start : part + start + lanes] = low
                    target[at, 2 * part + start : 2 * part + start + lanes] = high
            for fold, at in enumerate(columns):
                for k in range(HISTORY):
                    history[rows, k * FFT + at : k * FFT + at + lanes] = past[fold][k]
        return carry

    lax.fori_loop(0, inputs_here // ROWS, filter_rows, 0)

    for (_, channels), transform, source in zip(groups, transforms, folded):
        per_channel = transform.shape[0] // len(channels)
        batch = max(1, min(FRAME_BLOCK, 256 // inputs_here)) if inputs_here >= lanes else 1
        for first in range(0, FRAME_BLOCK, batch):
            result = lax.dot_general(
                transform[...],
                source[first * inputs_here : (first + batch) * inputs_here, :],
                (((1,), (1,)), ((), ())),
                preferred_element_type=jnp.float32,
            )
            for frame in range(batch):
                turned[pl.ds(first + frame, transform.shape[0], stride=FRAME_BLOCK), :] = result[
                    :, frame * inputs_here : (frame + 1) * inputs_here
                ]
        for index, channel in enumerate(channels):
            start = index * per_channel * FRAME_BLOCK
            block = turned[start : start + per_channel * FRAME_BLOCK, :]
            chunk, slot = places[channel]
            block = block.reshape(per_channel // 2, 2, FRAME_BLOCK, inputs_here)
            outputs[chunk][:, slot] = block.astype(jnp.bfloat16)


def spectra(voltages, history, first_block, blocks, arrays, devices, chan_local):
    folds = 2 if chan_local % 2 == 0 else 1
    inputs_here = voltages.shape[0]
    places = {}
    groups = []
    for index, (channels, _, _, _, _) in enumerate(arrays):
        places.update({channel: (index, slot) for slot, channel in enumerate(channels)})
    for residue in range(folds):
        members = [channel for channel in sorted(places) if channel % folds == residue]
        if members:
            groups.append((residue, members))
    transforms = [jnp.asarray(build_transform(members, devices, chan_local, folds)) for _, members in groups]
    depth = 3 * (FFT // folds)
    most = max(transform.shape[0] for transform in transforms)
    existing = [(index, array[4]) for index, array in enumerate(arrays) if array[4] is not None]
    operand_count = 2 + len(history) + len(transforms)
    frames = blocks * FRAME_BLOCK
    return pl.pallas_call(
        functools.partial(spectra_kernel, groups, folds, places, len(history), len(arrays)),
        grid=(blocks,),
        in_specs=[pl.BlockSpec((inputs_here, FRAME_BLOCK * FFT), lambda step: (0, first_block + step))]
        + history_specs(history, inputs_here, first_block)
        + [pl.BlockSpec((TAPS, FFT), lambda step: (0, 0))]
        + [pl.BlockSpec(transform.shape, lambda step: (0, 0)) for transform in transforms]
        + [pl.BlockSpec(memory_space=pl.ANY) for _ in existing],
        out_specs=[
            pl.BlockSpec(
                (devices, len(channels), 2, FRAME_BLOCK, inputs_here),
                place,
            )
            for channels, _, _, place, _ in arrays
        ],
        out_shape=[
            jax.ShapeDtypeStruct((devices, units, 2, unit_frames, inputs_here), jnp.bfloat16)
            for _, units, unit_frames, _, _ in arrays
        ],
        input_output_aliases={operand_count + k: index for k, (index, _) in enumerate(existing)},
        scratch_shapes=[
            pltpu.VMEM((inputs_here, HISTORY * FFT), jnp.float32),
            pltpu.VMEM((most * FRAME_BLOCK, inputs_here), jnp.float32),
        ]
        + [pltpu.VMEM((FRAME_BLOCK * inputs_here, depth), jnp.bfloat16) for _ in groups],
        compiler_params=pltpu.CompilerParams(vmem_limit_bytes=VMEM_LIMIT),
        cost_estimate=pl.CostEstimate(
            flops=2 * frames * inputs_here * depth * sum(transform.shape[0] for transform in transforms),
            bytes_accessed=frames * inputs_here * (4 * FFT + 4 * devices * len(places)),
            transcendentals=0,
        ),
        name="spectra",
    )(
        voltages,
        *history,
        jnp.asarray(build_taps().astype(np.float32)),
        *transforms,
        *[array for _, array in existing],
    )


def visibility_kernel(piece_units, carried, *refs):
    pieces = refs[: len(piece_units)]
    across, turned, swapped, above = refs[-4:]
    real_out, imag_out = refs[-6 - carried : -4 - carried][:2]
    total_frames = across.shape[0] // 2
    row_block, inputs = real_out.shape[1:]

    @pl.when(pl.program_id(1) == 0)
    def _():
        top = 0
        for piece, units in zip(pieces, piece_units):
            chan_count, blk_count, _, _, frames, inputs_here = piece.shape
            for blk in range(blk_count):
                for unit in units:
                    for part in range(2):
                        rows = slice(part * total_frames + top, part * total_frames + top + frames)
                        for chan in range(chan_count):
                            columns = slice(chan * inputs_here, (chan + 1) * inputs_here)
                            across[rows, columns] = piece[chan, blk, unit, part]
                    top += frames

    def one_block(step):
        start = step * row_block
        turned[...] = across[:, start : start + row_block].T
        swapped[:, :total_frames] = turned[:, total_frames:]
        swapped[:, total_frames:] = -turned[:, :total_frames]
        columns = across[:, start:]
        for index, (rows, output) in enumerate(((turned, real_out), (swapped, imag_out))):
            result = jnp.dot(rows[...], columns, preferred_element_type=jnp.float32) / total_frames
            output[0, :, start:] = result
            if start + row_block < inputs:
                above[index, start : start + row_block, start + row_block :] = result[:, row_block:]
            for left in range(0, start, row_block):
                mirrored = above[index, left : left + row_block, start : start + row_block].T
                output[0, :, left : left + row_block] = mirrored if index == 0 else -mirrored

    for step in range(inputs // row_block):
        pl.when(pl.program_id(1) == step)(functools.partial(one_block, step))


def visibilities(pieces, channels, before, carry, chan_local, in_vmem=False):
    arrays = [array for array, _ in pieces]
    piece_units = [units or [0] for _, units in pieces]
    chan_count, blk_count, _, _, _, inputs_here = arrays[0].shape
    inputs = chan_count * inputs_here
    depth = sum(blk_count * 2 * array.shape[4] * len(units) for array, units in zip(arrays, piece_units))
    row_block = 256
    shape = jax.ShapeDtypeStruct((chan_local, inputs, inputs), jnp.float32)
    out_spec = pl.BlockSpec((1, row_block, inputs), lambda channel, step: (channels[0] + channel, step, 0))
    anywhere = pl.BlockSpec(memory_space=pl.ANY)
    aliases = {len(arrays) + index: index for index in range(len(before))}
    aliases.update({len(arrays) + len(before) + index: 2 + index for index in range(len(carry))})
    piece_specs = []
    for array, units in pieces:
        if in_vmem:
            piece_specs.append(pl.BlockSpec(memory_space=pltpu.VMEM))
        elif units:
            piece_specs.append(pl.BlockSpec(array.shape, lambda channel, step: (0, 0, 0, 0, 0, 0)))
        else:
            block = (chan_count, blk_count, 1) + array.shape[3:]
            piece_specs.append(pl.BlockSpec(block, lambda channel, step: (0, 0, channel, 0, 0, 0)))
    results = pl.pallas_call(
        functools.partial(visibility_kernel, piece_units, len(carry)),
        grid=(len(channels), inputs // row_block),
        in_specs=piece_specs + [anywhere for _ in before] + [anywhere for _ in carry],
        out_specs=[out_spec, out_spec] + [anywhere for _ in carry],
        out_shape=[shape, shape] + [jax.ShapeDtypeStruct(array.shape, array.dtype) for array in carry],
        input_output_aliases=aliases,
        scratch_shapes=[
            pltpu.VMEM((depth, inputs), jnp.bfloat16),
            pltpu.VMEM((row_block, depth), jnp.bfloat16),
            pltpu.VMEM((row_block, depth), jnp.bfloat16),
            pltpu.VMEM((2, inputs, inputs), jnp.float32),
        ],
        compiler_params=pltpu.CompilerParams(vmem_limit_bytes=VISIBILITY_LIMIT),
        cost_estimate=pl.CostEstimate(
            flops=4 * len(channels) * inputs * inputs * depth,
            bytes_accessed=len(channels) * (2 * depth * inputs + 8 * inputs * inputs),
            transcendentals=0,
        ),
        name="visibilities",
    )(*arrays, *before, *carry)
    return tuple(results[:2]), list(results[2:])


def local(voltages):
    inputs_here = voltages.shape[0]
    frames_dev = voltages.shape[1] // FFT
    chan_count = lax.axis_size("chan")
    blk_count = lax.axis_size("blk")
    devices = chan_count * blk_count
    chan_local = NC // devices
    blocks = frames_dev // FRAME_BLOCK
    upper = blocks * 5 // 8
    lower = blocks - upper

    def exchange(array):
        arrived = lax.all_to_all(array, ("chan", "blk"), split_axis=0, concat_axis=0, tiled=True)
        return arrived.reshape(chan_count, blk_count, *array.shape[1:])

    def frame_by_frame(step):
        return (0, 0, 0, step, 0)

    def unit_by_unit(first, step):
        return (0, first + step, 0, 0, 0)

    if chan_local < 4 or chan_local % 2 or upper == 0:
        tail = voltages[:, (frames_dev - HISTORY) * FFT :].astype(jnp.bfloat16)
        halo = shifted(tail, "blk", 1)
        outputs = ()
        arrays = [([channel], 1, frames_dev, frame_by_frame, None) for channel in range(chan_local)]
        for channel, array in enumerate(spectra(voltages, [halo], 0, blocks, arrays, devices, chan_local)):
            outputs, _ = visibilities([(exchange(array), None)], [channel], outputs, [], chan_local)
        return outputs

    first, second, last = 0, 2, 1
    rest = list(range(3, chan_local))
    early, tail = direct_spectra(
        voltages, first, lower, 1, upper * FRAME_BLOCK, frame_by_frame, devices, chan_local
    )
    halo = shifted(tail, "blk", 1)
    units = 2 * lower + upper
    above = functools.partial(unit_by_unit, 2 * lower)
    below = functools.partial(unit_by_unit, 0)
    pair, _ = direct_spectra(voltages, second, lower, units, FRAME_BLOCK, above, devices, chan_local)
    (pair,) = spectra(
        voltages, [halo], 0, lower, [([first, second], units, FRAME_BLOCK, below, pair)], devices, chan_local
    )
    many, final = spectra(
        voltages,
        [halo],
        0,
        blocks,
        [(rest, len(rest), frames_dev, frame_by_frame, None), ([last], 1, frames_dev, frame_by_frame, None)],
        devices,
        chan_local,
    )
    early = exchange(early)
    pair = exchange(pair)
    many = exchange(many)
    first_units = list(range(0, 2 * lower, 2))
    second_units = list(range(1, 2 * lower, 2)) + list(range(2 * lower, units))
    outputs, _ = visibilities([(early, [0]), (pair, first_units)], [first], (), [], chan_local)
    outputs, (final,) = visibilities([(pair, second_units)], [second], outputs, [final], chan_local)
    final = exchange(final)
    outputs, _ = visibilities([(many, None)], rest, outputs, [], chan_local)
    outputs, _ = visibilities([(final, None)], [last], outputs, [], chan_local, in_vmem=True)
    return outputs


def solution(mesh):
    return jax.shard_map(
        local,
        mesh=mesh,
        in_specs=(P("chan", "blk"),),
        out_specs=(P(("chan", "blk"), None, None), P(("chan", "blk"), None, None)),
        check_vma=False,
    )
```

```python
import functools

import jax
import jax.numpy as jnp
import numpy as np
from jax import lax
from jax.experimental import pallas as pl
from jax.experimental.pallas import tpu as pltpu
from jax.sharding import PartitionSpec as P

NC = 256
TAPS = 4
FFT = 512
HISTORY = TAPS - 1
FRAME_BLOCK = 16
ROWS = 16
DIRECT_LIMIT = 56 * 1024 * 1024
VMEM_LIMIT = 40 * 1024 * 1024
VISIBILITY_LIMIT = 40 * 1024 * 1024


def shifted(value, axis, steps):
    count = lax.axis_size(axis)
    leading, last = (max(0, -steps), min(count, count - steps))
    return lax.ppermute(value, axis, [(source, source + steps) for source in range(leading, last)])


def build_taps():
    length = TAPS * FFT
    points = np.arange(length, dtype=np.float64)
    window = 0.54 - 0.46 * np.cos(2.0 * np.pi * points / (length - 1))
    return (np.sinc((points - (length - 1) / 2.0) / FFT) * window).reshape(TAPS, FFT)


def spectrum_scale(filter_taps):
    energy = np.mean(np.sum(filter_taps * filter_taps, axis=0))
    return 1.0 / (56.0 * np.sqrt(FFT * energy))


def build_dft(channels, devices, chan_local, points):
    rows = []
    for channel in channels:
        whole = np.arange(devices) * chan_local + channel
        angle = (whole[:, None] * np.arange(points)[None, :] % FFT) * (2.0 * np.pi / FFT)
        rows.append(np.stack([np.cos(angle), -np.sin(angle)], axis=1))
    return (np.concatenate(rows) * spectrum_scale(build_taps())).reshape(-1, points)


def split_high_low(matrix):
    matrix = matrix.astype(np.float32)
    high = matrix.astype(jnp.bfloat16)
    return high, (matrix - high.astype(np.float32)).astype(jnp.bfloat16)


def build_transform(channels, devices, chan_local, folds):
    high, low = split_high_low(build_dft(channels, devices, chan_local, FFT // folds))
    return np.concatenate([high, high, low], axis=1)


def build_direct(channel, devices, chan_local):
    matrix = build_dft([channel], devices, chan_local, FFT)
    parts = [part for taps in build_taps() for part in split_high_low(matrix * taps[None, :])]
    return np.ascontiguousarray(np.concatenate(parts, axis=0).T)


def history_specs(history, inputs_here, first_block):
    if len(history) == 1:
        return [pl.BlockSpec((inputs_here, HISTORY * FFT), lambda step: (0, 0))]
    before = first_block * FRAME_BLOCK - HISTORY
    return [pl.BlockSpec((inputs_here, FFT), functools.partial(lambda at, step: (0, at), before + k)) for k in range(HISTORY)]


def direct_kernel(history_count, voltages, *refs):
    history = refs[:history_count]
    transform, output, tail, products, turned = refs[history_count:]
    inputs_here = voltages.shape[0]
    rows = turned.shape[0] // FRAME_BLOCK
    batch = 2 if inputs_here == 128 else 1

    newest = TAPS - 1

    def multiply(frames):
        samples = jnp.concatenate([source[:, at : at + FFT] for source, at in frames], axis=0)
        samples = samples.astype(jnp.float32).astype(jnp.bfloat16)
        result = jnp.dot(samples, transform[...], preferred_element_type=jnp.float32)
        return [result[k * inputs_here : (k + 1) * inputs_here] for k in range(len(frames))]

    @pl.when(pl.program_id(0) == 0)
    def _():
        for k, source in enumerate(history):
            products[k] = multiply([(source, 0)])[0][:, : 2 * newest * rows]

    for first in range(0, FRAME_BLOCK, batch):
        frames = range(first, first + batch)
        for frame, product in zip(frames, multiply([(voltages, frame * FFT) for frame in frames])):
            products[HISTORY + frame] = product[:, : 2 * newest * rows]
            total = product[:, 2 * newest * rows :]
            for offset in range(newest):
                total = total + products[frame + offset, :, 2 * offset * rows : 2 * (offset + 1) * rows]
            total = total.T
            turned[pl.ds(frame, rows, stride=FRAME_BLOCK), :] = total[:rows] + total[rows:]
    for frame in range(HISTORY):
        products[frame] = products[FRAME_BLOCK + frame]
    output[...] = turned[...].reshape(output.shape).astype(jnp.bfloat16)

    @pl.when(pl.program_id(0) == pl.num_programs(0) - 1)
    def _():
        tail[...] = voltages[:, (FRAME_BLOCK - HISTORY) * FFT :].astype(jnp.float32).astype(jnp.bfloat16)


def direct_spectra(voltages, channel, first_block, units, unit_frames, place, devices, chan_local):
    inputs_here = voltages.shape[0]
    frames = voltages.shape[1] // FFT - first_block * FRAME_BLOCK
    transform = jnp.asarray(build_direct(channel, devices, chan_local))
    history = [voltages] * HISTORY
    return pl.pallas_call(
        functools.partial(direct_kernel, len(history)),
        grid=(frames // FRAME_BLOCK,),
        in_specs=[pl.BlockSpec((inputs_here, FRAME_BLOCK * FFT), lambda step: (0, first_block + step))]
        + history_specs(history, inputs_here, first_block)
        + [pl.BlockSpec(transform.shape, lambda step: (0, 0))],
        out_specs=[
            pl.BlockSpec((devices, 1, 2, FRAME_BLOCK, inputs_here), place),
            pl.BlockSpec((inputs_here, HISTORY * FFT), lambda step: (0, 0)),
        ],
        out_shape=[
            jax.ShapeDtypeStruct((devices, units, 2, unit_frames, inputs_here), jnp.bfloat16),
            jax.ShapeDtypeStruct((inputs_here, HISTORY * FFT), jnp.bfloat16),
        ],
        scratch_shapes=[
            pltpu.VMEM((HISTORY + FRAME_BLOCK, inputs_here, transform.shape[1] // TAPS * (TAPS - 1)), jnp.float32),
            pltpu.VMEM((devices * 2 * FRAME_BLOCK, inputs_here), jnp.float32),
        ],
        compiler_params=pltpu.CompilerParams(vmem_limit_bytes=DIRECT_LIMIT),
        cost_estimate=pl.CostEstimate(
            flops=2 * frames * inputs_here * FFT * transform.shape[1],
            bytes_accessed=frames * inputs_here * (4 * FFT + 4 * devices),
            transcendentals=0,
        ),
        name="direct_spectra",
    )(voltages, *history, transform)


def spectra_kernel(groups, folds, places, history_count, array_count, voltages, *refs):
    before = refs[:history_count]
    taps = refs[history_count]
    transforms = refs[history_count + 1 : history_count + 1 + len(groups)]
    history, turned = refs[-2 - len(groups) : len(refs) - len(groups)]
    folded = refs[len(refs) - len(groups) :]
    outputs = refs[-2 - len(groups) - array_count : -2 - len(groups)]
    inputs_here = voltages.shape[0]
    part = FFT // folds
    lanes = 128

    @pl.when(pl.program_id(0) == 0)
    def _():
        at = 0
        for source in before:
            history[:, at : at + source.shape[1]] = source[...].astype(jnp.float32)
            at += source.shape[1]

    def filter_rows(step, carry):
        rows = pl.ds(pl.multiple_of(step * ROWS, ROWS), ROWS)
        for start in range(0, part, lanes):
            columns = [fold * part + start for fold in range(folds)]
            weights = [[taps[offset : offset + 1, at : at + lanes] for offset in range(TAPS)] for at in columns]
            past = [[history[rows, k * FFT + at : k * FFT + at + lanes] for k in range(HISTORY)] for at in columns]
            for frame in range(FRAME_BLOCK):
                filtered = []
                for fold, column in enumerate(columns):
                    at = frame * FFT + column
                    past[fold].append(voltages[rows, at : at + lanes].astype(jnp.float32))
                    value = weights[fold][0] * past[fold].pop(0)
                    for offset in range(1, TAPS):
                        value = value + weights[fold][offset] * past[fold][offset - 1]
                    filtered.append(value)
                for (residue, _), target in zip(groups, folded):
                    value = filtered[0]
                    if folds == 2:
                        value = value + filtered[1] if residue == 0 else value - filtered[1]
                    high = value.astype(jnp.bfloat16)
                    low = (value - high.astype(jnp.float32)).astype(jnp.bfloat16)
                    at = pl.ds(pl.multiple_of(frame * inputs_here + step * ROWS, ROWS), ROWS)
                    target[at, start : start + lanes] = high
                    target[at, part + start : part + start + lanes] = low
                    target[at, 2 * part + start : 2 * part + start + lanes] = high
            for fold, at in enumerate(columns):
                for k in range(HISTORY):
                    history[rows, k * FFT + at : k * FFT + at + lanes] = past[fold][k]
        return carry

    lax.fori_loop(0, inputs_here // ROWS, filter_rows, 0)

    for (_, channels), transform, source in zip(groups, transforms, folded):
        per_channel = transform.shape[0] // len(channels)
        batch = max(1, min(FRAME_BLOCK, 256 // inputs_here)) if inputs_here >= lanes else 1
        for first in range(0, FRAME_BLOCK, batch):
            result = lax.dot_general(
                transform[...],
                source[first * inputs_here : (first + batch) * inputs_here, :],
                (((1,), (1,)), ((), ())),
                preferred_element_type=jnp.float32,
            )
            for frame in range(batch):
                turned[pl.ds(first + frame, transform.shape[0], stride=FRAME_BLOCK), :] = result[
                    :, frame * inputs_here : (frame + 1) * inputs_here
                ]
        for index, channel in enumerate(channels):
            start = index * per_channel * FRAME_BLOCK
            block = turned[start : start + per_channel * FRAME_BLOCK, :]
            chunk, slot = places[channel]
            block = block.reshape(per_channel // 2, 2, FRAME_BLOCK, inputs_here)
            outputs[chunk][:, slot] = block.astype(jnp.bfloat16)


def spectra(voltages, history, first_block, blocks, arrays, devices, chan_local):
    folds = 2 if chan_local % 2 == 0 else 1
    inputs_here = voltages.shape[0]
    places = {}
    groups = []
    for index, (channels, _, _, _, _) in enumerate(arrays):
        places.update({channel: (index, slot) for slot, channel in enumerate(channels)})
    for residue in range(folds):
        members = [channel for channel in sorted(places) if channel % folds == residue]
        if members:
            groups.append((residue, members))
    transforms = [jnp.asarray(build_transform(members, devices, chan_local, folds)) for _, members in groups]
    depth = 3 * (FFT // folds)
    most = max(transform.shape[0] for transform in transforms)
    existing = [(index, array[4]) for index, array in enumerate(arrays) if array[4] is not None]
    operand_count = 2 + len(history) + len(transforms)
    frames = blocks * FRAME_BLOCK
    return pl.pallas_call(
        functools.partial(spectra_kernel, groups, folds, places, len(history), len(arrays)),
        grid=(blocks,),
        in_specs=[pl.BlockSpec((inputs_here, FRAME_BLOCK * FFT), lambda step: (0, first_block + step))]
        + history_specs(history, inputs_here, first_block)
        + [pl.BlockSpec((TAPS, FFT), lambda step: (0, 0))]
        + [pl.BlockSpec(transform.shape, lambda step: (0, 0)) for transform in transforms]
        + [pl.BlockSpec(memory_space=pl.ANY) for _ in existing],
        out_specs=[
            pl.BlockSpec(
                (devices, len(channels), 2, FRAME_BLOCK, inputs_here),
                place,
            )
            for channels, _, _, place, _ in arrays
        ],
        out_shape=[
            jax.ShapeDtypeStruct((devices, units, 2, unit_frames, inputs_here), jnp.bfloat16)
            for _, units, unit_frames, _, _ in arrays
        ],
        input_output_aliases={operand_count + k: index for k, (index, _) in enumerate(existing)},
        scratch_shapes=[
            pltpu.VMEM((inputs_here, HISTORY * FFT), jnp.float32),
            pltpu.VMEM((most * FRAME_BLOCK, inputs_here), jnp.float32),
        ]
        + [pltpu.VMEM((FRAME_BLOCK * inputs_here, depth), jnp.bfloat16) for _ in groups],
        compiler_params=pltpu.CompilerParams(vmem_limit_bytes=VMEM_LIMIT),
        cost_estimate=pl.CostEstimate(
            flops=2 * frames * inputs_here * depth * sum(transform.shape[0] for transform in transforms),
            bytes_accessed=frames * inputs_here * (4 * FFT + 4 * devices * len(places)),
            transcendentals=0,
        ),
        name="spectra",
    )(
        voltages,
        *history,
        jnp.asarray(build_taps().astype(np.float32)),
        *transforms,
        *[array for _, array in existing],
    )


def visibility_kernel(piece_units, carried, *refs):
    pieces = refs[: len(piece_units)]
    across, turned, swapped, above = refs[-4:]
    real_out, imag_out = refs[-6 - carried : -4 - carried][:2]
    total_frames = across.shape[0] // 2
    row_block, inputs = real_out.shape[1:]

    @pl.when(pl.program_id(1) == 0)
    def _():
        top = 0
        for piece, units in zip(pieces, piece_units):
            chan_count, blk_count, _, _, frames, inputs_here = piece.shape
            for blk in range(blk_count):
                for unit in units:
                    for part in range(2):
                        rows = slice(part * total_frames + top, part * total_frames + top + frames)
                        for chan in range(chan_count):
                            columns = slice(chan * inputs_here, (chan + 1) * inputs_here)
                            across[rows, columns] = piece[chan, blk, unit, part]
                    top += frames

    def one_block(step):
        start = step * row_block
        turned[...] = across[:, start : start + row_block].T
        swapped[:, :total_frames] = turned[:, total_frames:]
        swapped[:, total_frames:] = -turned[:, :total_frames]
        columns = across[:, start:]
        for index, (rows, output) in enumerate(((turned, real_out), (swapped, imag_out))):
            result = jnp.dot(rows[...], columns, preferred_element_type=jnp.float32) / total_frames
            output[0, :, start:] = result
            if start + row_block < inputs:
                above[index, start : start + row_block, start + row_block :] = result[:, row_block:]
            for left in range(0, start, row_block):
                mirrored = above[index, left : left + row_block, start : start + row_block].T
                output[0, :, left : left + row_block] = mirrored if index == 0 else -mirrored

    for step in range(inputs // row_block):
        pl.when(pl.program_id(1) == step)(functools.partial(one_block, step))


def visibilities(pieces, channels, before, carry, chan_local, in_vmem=False):
    arrays = [array for array, _ in pieces]
    piece_units = [units or [0] for _, units in pieces]
    chan_count, blk_count, _, _, _, inputs_here = arrays[0].shape
    inputs = chan_count * inputs_here
    depth = sum(blk_count * 2 * array.shape[4] * len(units) for array, units in zip(arrays, piece_units))
    row_block = 256
    shape = jax.ShapeDtypeStruct((chan_local, inputs, inputs), jnp.float32)
    out_spec = pl.BlockSpec((1, row_block, inputs), lambda channel, step: (channels[0] + channel, step, 0))
    anywhere = pl.BlockSpec(memory_space=pl.ANY)
    aliases = {len(arrays) + index: index for index in range(len(before))}
    aliases.update({len(arrays) + len(before) + index: 2 + index for index in range(len(carry))})
    piece_specs = []
    for array, units in pieces:
        if in_vmem:
            piece_specs.append(pl.BlockSpec(memory_space=pltpu.VMEM))
        elif units:
            piece_specs.append(pl.BlockSpec(array.shape, lambda channel, step: (0, 0, 0, 0, 0, 0)))
        else:
            block = (chan_count, blk_count, 1) + array.shape[3:]
            piece_specs.append(pl.BlockSpec(block, lambda channel, step: (0, 0, channel, 0, 0, 0)))
    results = pl.pallas_call(
        functools.partial(visibility_kernel, piece_units, len(carry)),
        grid=(len(channels), inputs // row_block),
        in_specs=piece_specs + [anywhere for _ in before] + [anywhere for _ in carry],
        out_specs=[out_spec, out_spec] + [anywhere for _ in carry],
        out_shape=[shape, shape] + [jax.ShapeDtypeStruct(array.shape, array.dtype) for array in carry],
        input_output_aliases=aliases,
        scratch_shapes=[
            pltpu.VMEM((depth, inputs), jnp.bfloat16),
            pltpu.VMEM((row_block, depth), jnp.bfloat16),
            pltpu.VMEM((row_block, depth), jnp.bfloat16),
            pltpu.VMEM((2, inputs, inputs), jnp.float32),
        ],
        compiler_params=pltpu.CompilerParams(vmem_limit_bytes=VISIBILITY_LIMIT),
        cost_estimate=pl.CostEstimate(
            flops=4 * len(channels) * inputs * inputs * depth,
            bytes_accessed=len(channels) * (2 * depth * inputs + 8 * inputs * inputs),
            transcendentals=0,
        ),
        name="visibilities",
    )(*arrays, *before, *carry)
    return tuple(results[:2]), list(results[2:])


def local(voltages):
    inputs_here = voltages.shape[0]
    frames_dev = voltages.shape[1] // FFT
    chan_count = lax.axis_size("chan")
    blk_count = lax.axis_size("blk")
    devices = chan_count * blk_count
    chan_local = NC // devices
    blocks = frames_dev // FRAME_BLOCK
    upper = blocks * 5 // 8
    lower = blocks - upper

    def exchange(array):
        arrived = lax.all_to_all(array, ("chan", "blk"), split_axis=0, concat_axis=0, tiled=True)
        return arrived.reshape(chan_count, blk_count, *array.shape[1:])

    def frame_by_frame(step):
        return (0, 0, 0, step, 0)

    def unit_by_unit(first, step):
        return (0, first + step, 0, 0, 0)

    if chan_local < 4 or chan_local % 2 or upper == 0:
        tail = voltages[:, (frames_dev - HISTORY) * FFT :].astype(jnp.bfloat16)
        halo = shifted(tail, "blk", 1)
        outputs = ()
        arrays = [([channel], 1, frames_dev, frame_by_frame, None) for channel in range(chan_local)]
        for channel, array in enumerate(spectra(voltages, [halo], 0, blocks, arrays, devices, chan_local)):
            outputs, _ = visibilities([(exchange(array), None)], [channel], outputs, [], chan_local)
        return outputs

    first, second, last = 0, 2, 1
    rest = list(range(3, chan_local))
    early, tail = direct_spectra(
        voltages, first, lower, 1, upper * FRAME_BLOCK, frame_by_frame, devices, chan_local
    )
    halo = shifted(tail, "blk", 1)
    units = 2 * lower + upper
    above = functools.partial(unit_by_unit, 2 * lower)
    below = functools.partial(unit_by_unit, 0)
    pair, _ = direct_spectra(voltages, second, lower, units, FRAME_BLOCK, above, devices, chan_local)
    (pair,) = spectra(
        voltages, [halo], 0, lower, [([first, second], units, FRAME_BLOCK, below, pair)], devices, chan_local
    )
    many, final = spectra(
        voltages,
        [halo],
        0,
        blocks,
        [(rest, len(rest), frames_dev, frame_by_frame, None), ([last], 1, frames_dev, frame_by_frame, None)],
        devices,
        chan_local,
    )
    early = exchange(early)
    pair = exchange(pair)
    many = exchange(many)
    first_units = list(range(0, 2 * lower, 2))
    second_units = list(range(1, 2 * lower, 2)) + list(range(2 * lower, units))
    outputs, _ = visibilities([(early, [0]), (pair, first_units)], [first], (), [], chan_local)
    outputs, (final,) = visibilities([(pair, second_units)], [second], outputs, [final], chan_local)
    final = exchange(final)
    outputs, _ = visibilities([(many, None)], rest, outputs, [], chan_local)
    outputs, _ = visibilities([(final, None)], [last], outputs, [], chan_local, in_vmem=True)
    return outputs


def solution(mesh):
    return jax.shard_map(
        local,
        mesh=mesh,
        in_specs=(P("chan", "blk"),),
        out_specs=(P(("chan", "blk"), None, None), P(("chan", "blk"), None, None)),
        check_vma=False,
    )
```
